256 devices in a mesh: seq: 64 (over z_hi, x, y), grp: 4 (over z_lo, core).
Axes of the slice: x: 4, y: 4, z: 8 (z_hi: 4, z_lo: 2; z = z_hi * 2 + z_lo), core: 2. Of those that a mesh axis runs over, the one named last changes fastest.
Arguments:
- block_query_rows: bfloat16 [4096, 8192], P(('seq', 'grp')), may hold values from -400 to 400
- block_key_rows: bfloat16 [4096, 1024], P(('seq', 'grp')), may hold values from -6 to 6
- block_value_rows: bfloat16 [4096, 1024], P(('seq', 'grp')), may hold values from -6 to 6
- stretch_pos: int32 [4096], replicated, may hold values from 0 to 4095, each once
- prompt_key_cache: bfloat16 [8192, 1024], P(('seq', 'grp')), may hold values from -6 to 6
- prompt_value_cache: bfloat16 [8192, 1024], P(('seq', 'grp')), may hold values from -6 to 6
- embed_table: bfloat16 [65536, 8192], P('grp', 'seq'), may hold values from -6 to 6
- query_weight: bfloat16 [8192, 8192], P('seq', 'grp'), may hold values from -64 to 64
- key_weight: bfloat16 [8192, 1024], P('seq', 'grp'), may hold values from -0.0625 to 0.0625
- value_weight: bfloat16 [8192, 1024], P('seq', 'grp'), may hold values from -0.0625 to 0.0625
- beam_tokens: int32 [128, 2], replicated, may hold values from 0 to 65535
- parent_beam: int32 [128], replicated, may hold values from 0 to 127
Outputs:
- stretch_attn: bfloat16 [4096, 8192], P('seq', 'grp')
- decode_attn: bfloat16 [128, 2, 8192], P('seq', None, 'grp')
The draws below stay inside these ranges and needn't reach their ends.
Inputs may be any that keep to these rules, and one draw needn't show every extreme that they name: `stretch_pos`: a permutation of 0 to 4095.
All inputs are finite; a program needn't handle non-finite values.
Results may differ from the reference program's by a relative error of at most 0.01155.
Values may be sent and summed in bfloat16 or wider, within the bound.
No kernel may reach another device: no remote copies, remote signals or barrier semaphores. Data moves between devices by JAX's collectives and lax.ppermute only.
A program may use at most 192 MiB of HBM per device.

```python
import math
import jax
import jax.numpy as jnp
import numpy as np
from jax import lax

MODEL_WIDTH = 8192
QUERY_HEADS = 64
KEY_VALUE_HEADS = 8
HEAD_SIZE = 128
VOCAB = 65536
BEAM_COUNT = 128
BLOCK_TOKENS = 4096
PREFIX_TOKENS = 8192


def common_keys(key):
    return jnp.clip(jax.random.normal(key, (PREFIX_TOKENS, KEY_VALUE_HEADS * HEAD_SIZE), jnp.float32), -6.0, 6.0)


def draw_prompt_key_cache(key, part):
    shared_prompt = common_keys(key)
    return shared_prompt.astype(jnp.bfloat16)


def draw_block_query_rows(key, part):
    key = jax.random.fold_in(key, 23)
    return jnp.clip(jax.random.normal(key, (BLOCK_TOKENS, QUERY_HEADS * HEAD_SIZE), jnp.float32), -6.0, 6.0).astype(jnp.bfloat16)


def draw_query_weight(key, part):
    key = jax.random.fold_in(key, 37)
    drawn_key = jax.random.fold_in(key, 0)
    drawn = jnp.clip(jax.random.normal(drawn_key, (MODEL_WIDTH, QUERY_HEADS * HEAD_SIZE), jnp.float32), -6.0, 6.0) * MODEL_WIDTH ** (-0.5)
    return drawn.astype(jnp.bfloat16)


def touch_ends(entries, own_key, smallest, largest):
    longest = entries.shape.index(max(entries.shape))
    spots = []
    for shift in (0, 1):
        where = [jax.random.randint(jax.random.fold_in(own_key, axis), (), 0, length) for axis, length in enumerate(entries.shape)]
        where[longest] = (where[longest] + shift) % entries.shape[longest]
        spots.append(tuple(where))
    return entries.at[spots[0]].set(smallest).at[spots[1]].set(largest)


def block_scale(stream_key, shape, cuts, smallest, high):
    def one(axis_at, parts):
        steps = jax.random.uniform(jax.random.fold_in(jax.random.fold_in(stream_key, 6), axis_at), (parts,), jnp.float32, smallest / len(cuts), high / len(cuts))
        return jnp.repeat(jnp.exp(steps), shape[axis_at] // parts).reshape((-1,) + (1,) * (len(shape) - axis_at - 1))

    factor_of = one(*cuts[0])
    for cut in cuts[1:]:
        factor_of = factor_of * one(*cut)
    return factor_of


def rank_bounds(count, skew):
    weights = [(1 << 20) // math.isqrt(rank ** skew) + 1 for rank in range(1, count + 1)]
    scale = 1 + sum(weights) // (1 << 30)
    return np.cumsum(np.array([max(1, weight // scale) for weight in weights]))


def ranked(key, dims, count, slope):
    table = rank_bounds(count, slope)
    ticket = jax.random.randint(jax.random.fold_in(key, 1), dims, 0, int(table[count - 1]))
    standing = jnp.searchsorted(jnp.asarray(table, jnp.int32), ticket, side="right")
    return jax.random.permutation(jax.random.fold_in(key, 2), count)[standing].astype(jnp.int32)


def gaussian(key, extent, width, reach, cuts=(), held_as=jnp.bfloat16):
    entries = jax.random.normal(key, extent, jnp.float32) * width
    if len(cuts) > 0:
        entries = block_scale(key, extent, cuts, -0.22, 0.18) * entries
    return jnp.clip(entries, min=-reach, max=reach).astype(held_as)


def setup_inputs(seed: int = 0) -> dict:
    splits = jax.random.split(jax.random.key(seed), 13)
    return {
        "block_query_rows": draw_block_query_rows(jax.random.fold_in(splits[12], 71), 0),
        "block_key_rows": gaussian(splits[1], (BLOCK_TOKENS, KEY_VALUE_HEADS * HEAD_SIZE), 1.0, 6.0, ((0, 256),)),
        "block_value_rows": gaussian(splits[2], (BLOCK_TOKENS, KEY_VALUE_HEADS * HEAD_SIZE), 1.0, 6.0, ((0, 256),)),
        "stretch_pos": jax.random.permutation(splits[3], BLOCK_TOKENS).astype(jnp.int32),
        "prompt_key_cache": draw_prompt_key_cache(jax.random.fold_in(splits[12], 71), 0),
        "prompt_value_cache": gaussian(splits[5], (PREFIX_TOKENS, KEY_VALUE_HEADS * HEAD_SIZE), 1.0, 6.0, ((0, 256),)),
        "embed_table": gaussian(splits[6], (VOCAB, MODEL_WIDTH), 1.0, 6.0, ((0, 4), (1, 64))),
        "query_weight": draw_query_weight(jax.random.fold_in(splits[12], 71), 0),
        "key_weight": gaussian(splits[8], (MODEL_WIDTH, KEY_VALUE_HEADS * HEAD_SIZE), MODEL_WIDTH ** -0.5, 0.0625, ((0, 64), (1, 4))),
        "value_weight": gaussian(splits[9], (MODEL_WIDTH, KEY_VALUE_HEADS * HEAD_SIZE), MODEL_WIDTH ** -0.5, 0.0625, ((0, 64), (1, 4))),
        "beam_tokens": touch_ends(ranked(splits[10], (BEAM_COUNT, 2), VOCAB, 2), jax.random.fold_in(splits[10], 3), 0, VOCAB - 1).astype(jnp.int32),
        "parent_beam": touch_ends(jax.random.randint(splits[11], (BEAM_COUNT,), 0, BEAM_COUNT), jax.random.fold_in(splits[11], 1), 0, BEAM_COUNT - 1).astype(jnp.int32),
    }


def settle(scores):
    top = jnp.max(scores, axis=-1, keepdims=True)
    weights = jnp.exp(scores - top)
    total = jnp.sum(weights, axis=-1, keepdims=True)
    rounded = lax.optimization_barrier(weights.astype(jnp.bfloat16))
    return rounded.astype(jnp.float32), total


def reference(block_query_rows, block_key_rows, block_value_rows, stretch_pos, prompt_key_cache, prompt_value_cache, embed_table, query_weight, key_weight, value_weight, beam_tokens, parent_beam):
    query_group = QUERY_HEADS // KEY_VALUE_HEADS
    scale = HEAD_SIZE ** -0.5
    context_key_rows = jnp.concatenate([prompt_key_cache, block_key_rows], 0).reshape(-1, KEY_VALUE_HEADS, HEAD_SIZE)
    context_value_rows = jnp.concatenate([prompt_value_cache, block_value_rows], 0).reshape(-1, KEY_VALUE_HEADS, HEAD_SIZE)
    query_rows = block_query_rows.reshape(BLOCK_TOKENS, KEY_VALUE_HEADS, query_group, HEAD_SIZE)
    block = math.gcd(BLOCK_TOKENS, 512)

    def stretch_block(index):
        start = (index * block).astype(jnp.int32)
        row_count = lax.dynamic_slice_in_dim(query_rows, start, block, 0)
        pos = lax.dynamic_slice_in_dim(stretch_pos, start, block, 0)
        allowed = jnp.concatenate([jnp.ones((block, PREFIX_TOKENS), bool), stretch_pos[None, :] <= pos[:, None]], 1)

        def single_head(head):
            query = row_count[:, head].astype(jnp.float32)
            scores = jnp.einsum('tgd,nd->tgn', query, context_key_rows[:, head].astype(jnp.float32)) * scale
            scores = jnp.where(allowed[:, None, :], scores, -jnp.inf)
            weights, total = settle(scores)
            mixed = jnp.einsum('tgn,nd->tgd', weights, context_value_rows[:, head].astype(jnp.float32))
            return mixed / total

        return jnp.transpose(lax.map(single_head, jnp.arange(KEY_VALUE_HEADS, dtype=jnp.int32)), (1, 0, 2, 3))

    stretch_out = lax.map(stretch_block, jnp.arange(BLOCK_TOKENS // block, dtype=jnp.int32))
    stretch_attn = stretch_out.reshape(BLOCK_TOKENS, QUERY_HEADS * HEAD_SIZE).astype(jnp.bfloat16)

    hidden_state = embed_table[beam_tokens].reshape(BEAM_COUNT * 2, MODEL_WIDTH)
    beam_query_rows = jnp.dot(hidden_state, query_weight, preferred_element_type=jnp.float32).astype(jnp.bfloat16).reshape(BEAM_COUNT, 2, KEY_VALUE_HEADS, query_group, HEAD_SIZE)
    beam_key_rows = jnp.dot(hidden_state, key_weight, preferred_element_type=jnp.float32).astype(jnp.bfloat16).reshape(BEAM_COUNT, 2, KEY_VALUE_HEADS * HEAD_SIZE)
    beam_value_rows = jnp.dot(hidden_state, value_weight, preferred_element_type=jnp.float32).astype(jnp.bfloat16).reshape(BEAM_COUNT, 2, KEY_VALUE_HEADS * HEAD_SIZE)
    first_step_key = jnp.stack([beam_key_rows[:, 0], beam_key_rows[parent_beam, 0]], 1)
    first_step_value = jnp.stack([beam_value_rows[:, 0], beam_value_rows[parent_beam, 0]], 1)
    extra_key_rows = jnp.stack([first_step_key, beam_key_rows], 2).reshape(BEAM_COUNT, 2, 2, KEY_VALUE_HEADS, HEAD_SIZE)
    extra_value_rows = jnp.stack([first_step_value, beam_value_rows], 2).reshape(BEAM_COUNT, 2, 2, KEY_VALUE_HEADS, HEAD_SIZE)
    valid = jnp.arange(2)[:, None] >= jnp.arange(2)[None, :]
    count = PREFIX_TOKENS + BLOCK_TOKENS

    def beam_head_view(head):
        query = beam_query_rows[:, :, head].astype(jnp.float32)
        shared_prompt = jnp.einsum('bsgd,nd->bsgn', query, context_key_rows[:, head].astype(jnp.float32)) * scale
        own = jnp.einsum('bsgd,bsjd->bsgj', query, extra_key_rows[:, :, :, head].astype(jnp.float32)) * scale
        own = jnp.where(valid[None, :, None, :], own, -jnp.inf)
        weights, total = settle(jnp.concatenate([shared_prompt, own], -1))
        mixed = jnp.einsum('bsgn,nd->bsgd', weights[..., :count], context_value_rows[:, head].astype(jnp.float32))
        mixed = mixed + jnp.einsum('bsgj,bsjd->bsgd', weights[..., count:], extra_value_rows[:, :, :, head].astype(jnp.float32))
        return mixed / total

    decode_attention = lax.map(beam_head_view, jnp.arange(KEY_VALUE_HEADS, dtype=jnp.int32))
    decode_attn = jnp.transpose(decode_attention, (1, 2, 0, 3, 4)).reshape(BEAM_COUNT, 2, QUERY_HEADS * HEAD_SIZE).astype(jnp.bfloat16)
    return stretch_attn, decode_attn
```

```python
import jax
import jax.numpy as jnp
from jax import lax
from jax.experimental import pallas as pl
from jax.experimental.pallas import tpu as pltpu
from jax.sharding import Mesh, PartitionSpec as P

HEAD_SIZE = 128
GROUP = 8
WIDTH = GROUP * HEAD_SIZE
SCALE = HEAD_SIZE ** (-0.5)
EXP2_SCALE = SCALE * 1.4426950408889634
HIDE = -1e30
PIECE_OLD = 128
PIECE_NEW = 64
PIECE = PIECE_OLD + PIECE_NEW
ALL = ("zh", "x", "y", "zl", "c")
SEQ = ("zh", "x", "y")
GRP = ("zl", "c")
DEPTH = ("zh", "zl")
SHIFTS = (1, 3, 2)


def dot_nt(a, b):
    return lax.dot_general(a, b, (((1,), (1,)), ((), ())), preferred_element_type=jnp.float32)


def dot_nn(a, b):
    return lax.dot_general(a, b, (((1,), (0,)), ((), ())), preferred_element_type=jnp.float32)


def rows_of(refs, low, high, lane):
    parts = [r[:, low:high, lane : lane + HEAD_SIZE] for r in refs]
    parts = [p.reshape(p.shape[0] * p.shape[1], HEAD_SIZE) for p in parts]
    return jnp.concatenate(parts, 0)


def absorb(state, scores, values):
    top, total, acc = state
    peak = top
    for s in scores:
        peak = jnp.maximum(peak, jnp.max(s, axis=-1, keepdims=True))
    alpha = jnp.exp2((top - peak) * EXP2_SCALE)
    total = total * alpha
    acc = acc * alpha
    for s, v in zip(scores, values):
        w = jnp.exp2((s - peak[:, :1]) * EXP2_SCALE)
        total = total + jnp.sum(w, axis=-1, keepdims=True)
        acc = acc + dot_nn(w.astype(jnp.bfloat16), v)
    return peak, total, acc


def stretch_kernel(first, last, q_ref, qpos_ref, kpos_ref, *refs):
    kv = refs[:4]
    refs = refs[4:]
    if first:
        m_in = l_in = a_in = None
    else:
        m_in, l_in, a_in = refs[:3]
        refs = refs[3:]
    if last:
        (o_ref, m_ref, l_ref, a_ref) = refs
    else:
        (m_ref, l_ref, a_ref) = refs
    rows = q_ref.shape[0]
    for step in range(2):
        pair = kv[2 * step : 2 * step + 2]
        k_old = rows_of(pair, 0, PIECE_OLD, 0)
        k_new = rows_of(pair, PIECE_OLD, PIECE, 0)
        v_old = rows_of(pair, 0, PIECE_OLD, HEAD_SIZE)
        v_new = rows_of(pair, PIECE_OLD, PIECE, HEAD_SIZE)
        bias = jnp.where(kpos_ref[step : step + 1, :] <= qpos_ref[...], 0.0, HIDE)
        for head in range(GROUP):
            cols = slice(head * HEAD_SIZE, (head + 1) * HEAD_SIZE)
            q = q_ref[:, cols]
            if step == 0 and first:
                state = (
                    jnp.full((rows, HEAD_SIZE), HIDE, jnp.float32),
                    jnp.zeros((rows, HEAD_SIZE), jnp.float32),
                    jnp.zeros((rows, HEAD_SIZE), jnp.float32),
                )
            elif step == 0:
                state = (m_in[:, cols], l_in[:, cols], a_in[:, cols])
            else:
                state = (m_ref[:, cols], l_ref[:, cols], a_ref[:, cols])
            top, total, acc = absorb(
                state, (dot_nt(q, k_old), dot_nt(q, k_new) + bias), (v_old, v_new)
            )
            if step == 1 and last:
                o_ref[:, cols] = (acc / total).astype(jnp.bfloat16)
            else:
                m_ref[:, cols] = top
                l_ref[:, cols] = total
                a_ref[:, cols] = acc


def stretch_call(first, last, q, qpos, kpos, kv, carry):
    rows = q.shape[0]
    shape = jax.ShapeDtypeStruct((rows, WIDTH), jnp.float32)
    scratch = []
    if last:
        out_shape = jax.ShapeDtypeStruct((rows, WIDTH), jnp.bfloat16)
        scratch = [pltpu.VMEM((rows, WIDTH), jnp.float32)] * 3
    else:
        out_shape = [shape] * 3
    keys = sum(p.shape[0] * p.shape[1] for p in kv)
    return pl.pallas_call(
        lambda *refs: stretch_kernel(first, last, *refs),
        out_shape=out_shape,
        scratch_shapes=scratch,
        cost_estimate=pl.CostEstimate(
            flops=4 * rows * WIDTH * keys,
            bytes_accessed=keys * 512,
            transcendentals=rows * GROUP * keys,
        ),
        compiler_params=pltpu.CompilerParams(vmem_limit_bytes=48 * 1024 * 1024),
        name="stretch",
    )(q, qpos, kpos, *kv, *carry)


def decode_kernel(count, q_ref, own_ref, *refs):
    kv = refs[:count]
    o_ref = refs[count]
    q = q_ref[...]
    rows = q.shape[0]
    state = (
        jnp.full((rows, HEAD_SIZE), HIDE, jnp.float32),
        jnp.zeros((rows, HEAD_SIZE), jnp.float32),
        jnp.zeros((rows, HEAD_SIZE), jnp.float32),
    )
    for at in range(0, count, 2):
        pair = kv[at : at + 2]
        k = rows_of(pair, 0, PIECE, 0)
        v = rows_of(pair, 0, PIECE, HEAD_SIZE)
        state = absorb(state, (dot_nt(q, k),), (v,))
    slots = own_ref.shape[0]
    row = lax.broadcasted_iota(jnp.int32, (rows, slots), 0)
    key = lax.broadcasted_iota(jnp.int32, (rows, slots), 1)
    step = (row // GROUP) % 2
    beam = row // (2 * GROUP)
    slot = key % 4
    first = jnp.logical_and(step == 0, slot == 0)
    second = jnp.logical_and(step == 1, jnp.logical_or(slot == 1, slot == 2))
    seen = jnp.logical_and(beam == key // 4, jnp.logical_or(first, second))
    own = jnp.where(seen, dot_nt(q, own_ref[:, :HEAD_SIZE]), HIDE)
    _, total, acc = absorb(state, (own,), (own_ref[:, HEAD_SIZE:],))
    o_ref[...] = (acc / total).astype(jnp.bfloat16)


def decode_call(q, own, kv):
    keys = sum(p.shape[0] * p.shape[1] for p in kv)
    rows = q.shape[0]
    return pl.pallas_call(
        lambda *refs: decode_kernel(len(kv), *refs),
        out_shape=jax.ShapeDtypeStruct((rows, HEAD_SIZE), jnp.bfloat16),
        cost_estimate=pl.CostEstimate(
            flops=4 * rows * HEAD_SIZE * keys, bytes_accessed=keys * 512, transcendentals=rows * keys
        ),
        compiler_params=pltpu.CompilerParams(vmem_limit_bytes=48 * 1024 * 1024),
        name="decode",
    )(q, own, *kv)


def shift(v, axis, size, by):
    return lax.ppermute(v, axis, [(i, (i + by) % size) for i in range(size)])


def swap_core(v):
    return lax.ppermute(v, "c", [(0, 1), (1, 0)])


def by_plane(v, unit):
    rows = v.shape[0]
    v = v.reshape(rows, 2, 2, 2, unit)
    return jnp.transpose(v, (3, 2, 1, 0, 4)).reshape(8, rows, unit)


def ring(table, start):
    return lax.dynamic_slice_in_dim(jnp.concatenate([table, table], 0), start, 4, 0)


def shards(
    block_query_rows,
    block_key_rows,
    block_value_rows,
    stretch_pos,
    prompt_key_cache,
    prompt_value_cache,
    embed_table,
    query_weight,
    key_weight,
    value_weight,
    beam_tokens,
    parent_beam,
):
    bf16 = jnp.bfloat16
    zh, xi, yi, ci = (lax.axis_index(a) for a in ("zh", "x", "y", "c"))

    keys = jnp.concatenate([prompt_key_cache, block_key_rows], 0)
    values = jnp.concatenate([prompt_value_cache, block_value_rows], 0)
    kv = jnp.concatenate([by_plane(keys, HEAD_SIZE), by_plane(values, HEAD_SIZE)], -1)
    kv = lax.all_to_all(kv, DEPTH, split_axis=0, concat_axis=0, tiled=True)
    q = by_plane(block_query_rows, WIDTH)
    q = lax.all_to_all(q, DEPTH, split_axis=0, concat_axis=0, tiled=True).reshape(-1, WIDTH)
    old_rows = prompt_key_cache.shape[0]
    half_a = jnp.concatenate(
        [kv[:4, :old_rows].reshape(PIECE_OLD, -1), kv[:4, old_rows:].reshape(PIECE_NEW, -1)], 0
    )
    half_b = jnp.concatenate(
        [kv[4:, :old_rows].reshape(PIECE_OLD, -1), kv[4:, old_rows:].reshape(PIECE_NEW, -1)], 0
    )

    line_a = jnp.stack([half_a] + [shift(half_a, "x", 4, k) for k in SHIFTS])
    line_b = jnp.stack([half_b] + [shift(half_b, "y", 4, k) for k in SHIFTS])
    rounds = [(line_a, line_b)]
    for k in SHIFTS:
        rounds.append((shift(line_a, "y", 4, k), shift(line_b, "x", 4, k)))
    pieces = [(a, b, swap_core(a), swap_core(b)) for a, b in rounds]

    pos = stretch_pos.reshape(4, 4, 4, 2, 2, -1)
    pos = jnp.transpose(pos, (1, 2, 4, 0, 3, 5)).reshape(4, 4, 2, 2, PIECE_NEW)
    pos = jnp.swapaxes(ring(jnp.swapaxes(ring(pos, xi), 0, 1), yi), 0, 1)
    pos = lax.dynamic_slice_in_dim(jnp.concatenate([pos, pos], 2), ci, 2, 2)
    qpos = pos[0, 0, 0].reshape(-1, 1)
    back = [0] + [(4 - k) % 4 for k in SHIFTS]

    def kpos_of(at):
        tables = []
        for core in range(2):
            row_a = [pos[bx, back[at], core, 0] for bx in back]
            row_b = [pos[back[at], by, core, 1] for by in back]
            tables.append(jnp.concatenate(row_a + row_b))
        return jnp.stack(tables)

    carry = ()
    for at in range(4):
        carry = stretch_call(at == 0, at == 3, q, qpos, kpos_of(at), pieces[at], carry)
    stretch = carry.reshape(4, -1, WIDTH)

    got = []
    for k in range(4):
        pairs = []
        for i in range(16):
            h1, h0, l, c = (i >> 3) & 1, (i >> 2) & 1, (i >> 1) & 1, i & 1
            pairs.append((i, (((2 * h1 + c + k) % 4) * 2 + l) * 2 + h0))
        mine = lax.dynamic_index_in_dim(stretch, (2 * (zh // 2) + ci + k) % 4, 0, keepdims=False)
        got.append(lax.ppermute(mine, ("zh", "zl", "c"), pairs))
    got = ring(jnp.stack(got), zh)
    got = jnp.stack([got[(4 - i) % 4] for i in range(4)])
    got = got.reshape(2, 2, 2, -1, WIDTH)
    stretch_attn = jnp.transpose(got, (2, 1, 3, 0, 4)).reshape(-1, 2 * WIDTH)

    vocab_rows = embed_table.shape[0]
    beams = beam_tokens.shape[0]
    local_ids = beam_tokens.reshape(-1) - lax.axis_index(GRP) * vocab_rows
    inside = jnp.logical_and(local_ids >= 0, local_ids < vocab_rows)
    looked = jnp.take(embed_table, jnp.clip(local_ids, 0, vocab_rows - 1), axis=0)
    hidden = jnp.where(inside[:, None], looked, jnp.zeros_like(looked))
    hidden = sum(
        [lax.ppermute(hidden, GRP, [(i, i ^ k) for i in range(4)]) for k in (1, 2, 3)], hidden
    )
    parent = jnp.take(hidden.reshape(beams, 2, -1)[:, 0], parent_beam, axis=0)
    rows3 = jnp.concatenate([hidden.reshape(beams, 2, -1), parent[:, None]], 1)

    depth = query_weight.shape[0]
    weights = jnp.concatenate(
        [w.reshape(depth, 4, -1) for w in (query_weight, key_weight, value_weight)], -1
    )
    weights = lax.all_to_all(
        jnp.transpose(weights, (1, 0, 2)), "x", split_axis=0, concat_axis=0, tiled=True
    )
    weights = weights.reshape(4 * depth, -1)
    wide = jnp.stack([rows3] + [shift(rows3, "x", 4, k) for k in SHIFTS])
    order = jnp.stack([wide[0], wide[2], wide[3], wide[1]])
    wide = ring(order, (4 - xi) % 4)
    wide = jnp.transpose(wide, (1, 2, 0, 3)).reshape(beams, 3, 4 * depth)
    q_cols = query_weight.shape[1] // 4
    part_q = jnp.einsum(
        "bsd,dc->bsc", wide[:, :2], weights[:, :q_cols], preferred_element_type=jnp.float32
    )
    part_kv = jnp.einsum(
        "bsd,dc->bsc", wide, weights[:, q_cols:], preferred_element_type=jnp.float32
    )
    share = beams // 16
    part = jnp.concatenate(
        [part_q.reshape(4, 4, share, -1), part_kv.reshape(4, 4, share, -1)], -1
    )
    part = jnp.sum(lax.all_to_all(part, "y", split_axis=1, concat_axis=1, tiled=True), axis=1)
    part = jnp.sum(lax.all_to_all(part, "zh", split_axis=0, concat_axis=0, tiled=True), axis=0)
    part = part.astype(bf16)

    halves = part.reshape(2, share // 2, -1)
    got = []
    for i in range(2):
        pairs = []
        for at in range(64):
            h, j, p, l, c = at >> 4, (at >> 3) & 1, (at >> 2) & 1, (at >> 1) & 1, at & 1
            pairs.append((at, (((2 * j + c) * 4 + h) * 2 + l) * 2 + (p ^ i)))
        mine = lax.dynamic_index_in_dim(halves, (xi % 2) ^ i, 0, keepdims=False)
        got.append(lax.ppermute(mine, ("zh", "x", "zl", "c"), pairs))
    even = ci == 0
    sides = (jnp.where(even, got[0], got[1]), jnp.where(even, got[1], got[0]))
    few = share // 2
    beam_q = jnp.stack([s[:, : 2 * q_cols].reshape(few, 2, 4, HEAD_SIZE) for s in sides], 2)
    beam_q = beam_q.reshape(few * 2 * GROUP, HEAD_SIZE)
    own = jnp.stack([s[:, 2 * q_cols :].reshape(few, 3, 2, HEAD_SIZE // 2) for s in sides], 3)
    own = own.reshape(few, 3, 2 * HEAD_SIZE)
    own = jnp.pad(own, ((0, 32 - few), (0, 1), (0, 0))).reshape(128, 2 * HEAD_SIZE)
    decode = decode_call(beam_q, own, [p for four in pieces for p in four])

    decode = decode.reshape(2, few // 2, 2, WIDTH)
    got = []
    for k in range(2):
        pairs = []
        for at in range(256):
            h1, h0, x, y = (at >> 7) & 1, (at >> 6) & 1, (at >> 4) & 3, (at >> 2) & 3
            l, c = (at >> 1) & 1, at & 1
            pairs.append((at, (((x * 4 + y) * 4 + 2 * c + (h1 ^ k)) * 2 + l) * 2 + h0))
        mine = lax.dynamic_index_in_dim(decode, (zh // 2) ^ k, 0, keepdims=False)
        got.append(lax.ppermute(mine, ALL, pairs))
    even = yi % 2 == 0
    sides = (jnp.where(even, got[0], got[1]), jnp.where(even, got[1], got[0]))
    decode_attn = jnp.concatenate(sides, -1)
    return stretch_attn, decode_attn


def solution(mesh):
    fine = Mesh(mesh.devices.reshape(4, 4, 4, 2, 2), ALL)
    return jax.shard_map(
        shards,
        mesh=fine,
        in_specs=(
            P(ALL, None),
            P(ALL, None),
            P(ALL, None),
            P(),
            P(ALL, None),
            P(ALL, None),
            P(GRP, SEQ),
            P(SEQ, GRP),
            P(SEQ, GRP),
            P(SEQ, GRP),
            P(),
            P(),
        ),
        out_specs=(P(SEQ, GRP), P(SEQ, None, GRP)),
        check_vma=False,
    )
```

```python
import jax
import jax.numpy as jnp
import numpy as np
from jax import lax
from jax.experimental import pallas as pl
from jax.experimental.pallas import tpu as pltpu
from jax.sharding import Mesh, PartitionSpec as P

HEAD = 128
GROUP = 8
WIDTH = GROUP * HEAD
EXP2_SCALE = HEAD ** (-0.5) * 1.4426950408889634
HIDE = -1e30
ALL = ("zh", "x", "y", "zl", "c")
SEQ = ("zh", "x", "y")
GRP = ("zl", "c")
DEPTH = ("zh", "zl")
OLD, NEW = 32, 16
BOTH = OLD + NEW
TOKENS = 8 * NEW
BEAMS = 8
TILES = 11 * BEAMS
ACC = WIDTH + TOKENS
STATE = ACC + 32
MESSAGE = 48
VMEM = pltpu.CompilerParams(vmem_limit_bytes=56 * 1024 * 1024)
SMEM_SPEC = pl.BlockSpec(memory_space=pltpu.SMEM)
VMEM_SPEC = pl.BlockSpec(memory_space=pltpu.VMEM)
BF16, F32 = jnp.bfloat16, jnp.float32


def dot_nt(a, b):
    return lax.dot_general(a, b, (((1,), (1,)), ((), ())), preferred_element_type=F32)


def dot_nn(a, b):
    return lax.dot_general(a, b, (((1,), (0,)), ((), ())), preferred_element_type=F32)


def call(kernel, out_shape, scalars, args, name, cost=None, scratch=()):
    return pl.pallas_call(
        kernel,
        out_shape=out_shape,
        in_specs=[SMEM_SPEC] * len(scalars) + [VMEM_SPEC] * len(args),
        out_specs=jax.tree.map(lambda _: VMEM_SPEC, out_shape),
        scratch_shapes=list(scratch),
        cost_estimate=cost,
        compiler_params=VMEM,
        name=name,
    )(*scalars, *args)


def head_of(plane):
    return 4 * (plane & 1) + 2 * ((plane >> 1) & 1) + (plane >> 2)


def pack_kv_kernel(old_k, old_v, new_k, new_v, out):
    for plane in range(8):
        cols = slice(head_of(plane) * HEAD, (head_of(plane) + 1) * HEAD)
        out[plane, :OLD, :HEAD] = old_k[:, cols]
        out[plane, :OLD, HEAD:] = old_v[:, cols]
        out[plane, OLD:, :HEAD] = new_k[:, cols]
        out[plane, OLD:, HEAD:] = new_v[:, cols]


def pack_q_kernel(q, out):
    for plane in range(8):
        for pair in range(4):
            at = head_of(plane) * WIDTH + pair * 2 * HEAD
            out[plane, pair * NEW : (pair + 1) * NEW, :] = q[:, at : at + 2 * HEAD]


def hidden_kernel(owner, parent, beam_id, looked, out):
    rows = jnp.zeros((looked.shape[1], HEAD), F32)
    for part in range(4):
        rows = rows + jnp.where(owner[...] == part, looked[part].astype(F32), 0.0)
    rows = rows.astype(BF16)
    half = rows.shape[0] // 2
    pick = jnp.where(parent[...] == beam_id[...], 1.0, 0.0).astype(BF16)
    extra = dot_nn(pick, rows[:half]).astype(BF16)
    for part in range(4):
        out[part, : 2 * half, :] = rows
        out[part, 2 * half :, :] = extra


def project_kernel(first, hidden, *refs):
    weights, (out, total) = refs[:4], refs[4:]
    acc = None
    for k in range(4):
        part = dot_nn(hidden[first[0] ^ k], weights[k][...])
        acc = part if acc is None else acc + part
    total[...] = acc
    count = total.shape[0] // 3
    for chip in range(16):
        y, x = chip // 4, chip % 4
        for step in range(3):
            rows = slice(step * count + chip * BEAMS, step * count + (chip + 1) * BEAMS)
            if step < 2:
                for head in range(4):
                    at = (step * 4 + head) * BEAMS
                    out[y, x, at : at + BEAMS, :] = total[rows, head * HEAD : (head + 1) * HEAD]
            at = (8 + step) * BEAMS
            out[y, x, at : at + BEAMS, :] = total[rows, 4 * HEAD :]


def sum_kernel(parts, out):
    out[...] = (parts[0] + parts[1]) + (parts[2] + parts[3])


def attend_kernel(core, pos, kv, q_own, q_other, mine, theirs, keep, send):
    me = core[0]
    per_step = 4
    steps = kv.shape[0] // per_step
    place = core[1]

    def column(which):
        row = pos[pl.ds(which * 16 + place, 1), :].astype(F32)
        return jnp.transpose(jnp.broadcast_to(row, (TOKENS, HEAD)))[:, :1]

    qpos = (column(me), column(1 - me))
    halves = [jnp.where(me == 0, mine[...], theirs[...]), jnp.where(me == 0, theirs[...], mine[...])]
    queries = jnp.concatenate([h[: 8 * BEAMS] for h in halves], 0).astype(BF16)

    def query(block):
        if block == 2 * GROUP:
            return queries
        source = q_own if block < GROUP else q_other
        head = block % GROUP
        rows = slice((head // 2) * NEW, (head // 2 + 1) * NEW)
        lanes = slice((head % 2) * HEAD, (head % 2 + 1) * HEAD)
        return source[:, rows, lanes].reshape(TOKENS, HEAD)

    tiles = {}

    def load(step):
        part = slice(step * per_step, (step + 1) * per_step)
        wide = []
        for low, high in ((0, OLD), (OLD, BOTH)):
            count = per_step * 8 * (high - low)
            k = kv[part, :, low:high, :HEAD].reshape(count, HEAD)
            v = kv[part, :, low:high, HEAD:].reshape(count, HEAD)
            wide.append((k, jnp.concatenate([v, jnp.ones_like(v)], 1)))
        rows = [pos[pl.ds(me * 16 + step * per_step + i, 1), :] for i in range(per_step)]
        kpos = jnp.concatenate(rows, 1).astype(F32)
        bias = [jnp.where(kpos <= p, 0.0, HIDE) for p in qpos]
        tiles[step] = (wide, bias)

    def scores(step, block):
        if step not in tiles:
            load(step)
        wide, bias = tiles[step]
        q = query(block)
        s_old = dot_nt(q, wide[0][0])
        s_new = dot_nt(q, wide[1][0])
        if block < 2 * GROUP:
            s_new = s_new + bias[block // GROUP]
        return s_old, s_new

    def places(block):
        if block < GROUP:
            return keep, block
        if block < 2 * GROUP:
            return send, block - GROUP
        return keep, GROUP

    def absorb(step, block, pair):
        ref, slot = places(block)
        rows = slice(slot * TOKENS, (slot + 1) * TOKENS)
        peak = jnp.maximum(
            jnp.max(pair[0], axis=-1, keepdims=True), jnp.max(pair[1], axis=-1, keepdims=True)
        )
        if step > 0:
            top, total, acc = state[block]
            peak = jnp.maximum(top, peak)
            alpha = jnp.exp2((top - peak) * EXP2_SCALE)
        else:
            peak = jnp.broadcast_to(peak, (TOKENS, HEAD))
        mixed = 0.0
        for s, (_, v) in zip(pair, tiles[step][0]):
            w = jnp.exp2((s - peak[:, :1]) * EXP2_SCALE).astype(BF16)
            mixed = mixed + dot_nn(w, v)
        acc_new, total_new = mixed[:, :HEAD], mixed[:, HEAD:]
        if step > 0:
            acc_new = acc_new + acc[...] * alpha
            total_new = total_new + total[...] * alpha
        return peak, total_new, acc_new

    state = {}
    order = [(step, block) for step in range(steps) for block in range(2 * GROUP + 1)]
    ahead = scores(*order[0])
    for i, (step, block) in enumerate(order):
        now = ahead
        if i + 1 < len(order):
            ahead = scores(*order[i + 1])
        state[block] = absorb(step, block, now)

    top, total, acc = state[2 * GROUP]
    count = 4 * BEAMS
    pad = jnp.zeros((count - 3 * BEAMS, HEAD), F32)
    own_k = jnp.concatenate([halves[0][8 * BEAMS :], pad], 0).astype(BF16)
    own_v = jnp.concatenate([halves[1][8 * BEAMS :], pad], 0).astype(BF16)
    row = lax.broadcasted_iota(jnp.int32, (TOKENS, count), 0)
    key = lax.broadcasted_iota(jnp.int32, (TOKENS, count), 1)
    step = (row // (4 * BEAMS)) % 2
    beam = row % BEAMS
    slot = key // BEAMS
    first = jnp.logical_and(step == 0, slot == 0)
    second = jnp.logical_and(step == 1, jnp.logical_or(slot == 1, slot == 2))
    seen = jnp.logical_and(beam == key % BEAMS, jnp.logical_or(first, second))
    seen = jnp.logical_and(seen, beam // 4 == me)
    own = jnp.where(seen, dot_nt(queries, own_k), HIDE)
    peak = jnp.maximum(top, jnp.max(own, axis=-1, keepdims=True))
    alpha = jnp.exp2((top - peak) * EXP2_SCALE)
    w = jnp.exp2((own - peak[:, :1]) * EXP2_SCALE)
    total = total * alpha + jnp.sum(w, axis=-1, keepdims=True)
    acc = acc * alpha + dot_nn(w.astype(BF16), own_v)
    state[2 * GROUP] = (peak, total, acc)

    for block in range(2 * GROUP + 1):
        ref, slot = places(block)
        top, total, acc = state[block]
        rows = slice(slot * TOKENS, (slot + 1) * TOKENS)
        top, total = jnp.transpose(top)[:1], jnp.transpose(total)[:1]
        for target in (keep, send) if block == 2 * GROUP else (ref,):
            target[rows, :] = acc
            target[ACC + slot : ACC + slot + 1, :] = top
            target[ACC + 16 + slot : ACC + 17 + slot, :] = total


def merge_kernel(core, keep, got, out, message):
    me, first = core[0], core[2]
    message[...] = jnp.zeros_like(message)

    def spread(ref, row):
        return jnp.transpose(jnp.broadcast_to(ref[row : row + 1, :], (TOKENS, HEAD)))

    for slot in range(GROUP + 1):
        rows = slice(slot * TOKENS, (slot + 1) * TOKENS)
        top_a, top_b = spread(keep, ACC + slot), spread(got, ACC + slot)
        peak = jnp.maximum(top_a, top_b)
        a, b = jnp.exp2((top_a - peak) * EXP2_SCALE), jnp.exp2((top_b - peak) * EXP2_SCALE)
        total = spread(keep, ACC + 16 + slot) * a + spread(got, ACC + 16 + slot) * b
        mixed = (keep[rows, :] * a + got[rows, :] * b) / total
        if slot < GROUP:
            lanes = slice(slot * HEAD, (slot + 1) * HEAD)
            for zh in range(4):
                message[zh, : 2 * NEW, lanes] = mixed[zh * 2 * NEW : (zh + 1) * 2 * NEW]
        else:
            for block in range(16):
                half, step, head = block // 8, (block // 4) % 2, block % 4
                lanes = slice((half * 4 + head) * HEAD, (half * 4 + head + 1) * HEAD)
                tile = mixed[block * BEAMS : (block + 1) * BEAMS]
                tile = jnp.where(me == 0, tile[:4], tile[4:])
                for zh in range(4):
                    message[zh, 2 * NEW + step : 2 * NEW + step + 1, lanes] = tile[zh : zh + 1]
    for k in range(4):
        out[k] = message[(first + k) % 4].astype(BF16)


def place_kernel(core, *refs):
    got, (stretch, decode) = refs[:4], refs[4:]
    zh = core[3]
    few = [jnp.zeros((2, WIDTH), F32)] * 4
    for k in range(4):
        origin = (zh - k + 4) % 4
        lane = pl.multiple_of((origin // 2) * WIDTH, WIDTH)
        for low in range(2):
            row = pl.multiple_of(low * 2 * NEW + (origin % 2) * NEW, NEW)
            stretch[pl.ds(row, NEW), pl.ds(lane, WIDTH)] = got[k][low * NEW : (low + 1) * NEW, :]
        tail = got[k][2 * NEW :, :].astype(F32)[:2]
        few = [jnp.where(origin == i, tail, f) for i, f in enumerate(few)]
    for i in range(4):
        head, parity = i // 2, i % 2
        decode[parity, :, head * WIDTH : (head + 1) * WIDTH] = few[i].astype(BF16)


def shards(
    block_query_rows,
    block_key_rows,
    block_value_rows,
    stretch_pos,
    prompt_key_cache,
    prompt_value_cache,
    embed_table,
    query_weight,
    key_weight,
    value_weight,
    beam_tokens,
    parent_beam,
):
    zh, xi, yi, ci = (lax.axis_index(a) for a in ("zh", "x", "y", "c"))
    core = jnp.stack([ci, xi * 4 + yi, 2 * (zh // 2) + ci, zh]).astype(jnp.int32)

    kv = call(
        pack_kv_kernel,
        jax.ShapeDtypeStruct((8, BOTH, 2 * HEAD), BF16),
        (),
        (prompt_key_cache, prompt_value_cache, block_key_rows, block_value_rows),
        "pack_kv",
    )
    kv = lax.all_to_all(kv, DEPTH, split_axis=0, concat_axis=0, tiled=True)
    kv = lax.all_gather(kv.reshape(8 * BOTH, 2 * HEAD), ("x", "y"), axis=0, tiled=True)
    kv = kv.reshape(16, 8, BOTH, 2 * HEAD)
    q = call(
        pack_q_kernel,
        jax.ShapeDtypeStruct((8, 4 * NEW, 2 * HEAD), BF16),
        (),
        (block_query_rows,),
        "pack_q",
    )
    q = lax.all_to_all(q, DEPTH, split_axis=0, concat_axis=0, tiled=True)
    q_other = lax.ppermute(q, "c", [(0, 1), (1, 0)])

    pos = jnp.transpose(stretch_pos.reshape(4, 4, 4, 2, 2, NEW), (4, 1, 2, 0, 3, 5))
    pos = pos.reshape(32, TOKENS)

    vocab_rows = embed_table.shape[0]
    beams = beam_tokens.shape[0]
    ids = jnp.transpose(beam_tokens.reshape(4, 4, 4, 2, 2), (4, 2, 1, 3, 0)).reshape(-1)
    looked = embed_table.at[ids % vocab_rows].get(mode="promise_in_bounds")
    looked = lax.all_to_all(
        jnp.broadcast_to(looked, (4,) + looked.shape), GRP, split_axis=0, concat_axis=0, tiled=True
    )
    beam_id = np.arange(beams, dtype=np.int32).reshape(4, 4, 4, 2).transpose(2, 1, 3, 0)
    parent = jnp.transpose(parent_beam.reshape(4, 4, 4, 2), (2, 1, 3, 0))
    hidden = call(
        hidden_kernel,
        jax.ShapeDtypeStruct((4, 3 * beams, HEAD), BF16),
        (),
        ((ids // vocab_rows)[:, None], parent.reshape(-1, 1), beam_id.reshape(1, -1), looked),
        "hidden",
    )
    hidden = lax.all_to_all(hidden, "zh", split_axis=0, concat_axis=0, tiled=True)

    depth = query_weight.shape[0]
    q_cols = query_weight.shape[1] // 4
    parts = jnp.concatenate(
        [
            query_weight.reshape(depth, 2, 2, q_cols),
            jnp.stack([key_weight.reshape(depth, 2, HEAD), value_weight.reshape(depth, 2, HEAD)], 2),
        ],
        -1,
    )
    parts = jnp.transpose(parts, (1, 2, 0, 3)).reshape(4, depth, q_cols + HEAD)
    weights = []
    for k in range(4):
        pairs = []
        for at in range(8):
            h, c = at // 2, at % 2
            to = h ^ k
            pairs.append((at, (2 * (to // 2) + c) * 2 + to % 2))
        mine = lax.dynamic_index_in_dim(parts, zh ^ k, 0, keepdims=False)
        weights.append(lax.ppermute(mine, ("zh", "c"), pairs))
    part = call(
        project_kernel,
        jax.ShapeDtypeStruct((4, 4, TILES, HEAD), F32),
        (core[2:3],),
        (hidden, *weights),
        "project",
        scratch=[pltpu.VMEM((3 * beams, q_cols + HEAD), F32)],
    )
    part = lax.all_to_all(part, "y", split_axis=0, concat_axis=0, tiled=True)
    part = call(sum_kernel, jax.ShapeDtypeStruct((4, TILES, HEAD), F32), (), (part,), "sum_y")
    part = lax.all_to_all(part, "x", split_axis=0, concat_axis=0, tiled=True)
    mine = call(sum_kernel, jax.ShapeDtypeStruct((TILES, HEAD), F32), (), (part,), "sum_x")
    theirs = lax.ppermute(mine, "c", [(0, 1), (1, 0)])

    rows = (2 * GROUP + 1) * TOKENS
    keys = 16 * 8 * BOTH
    state = jax.ShapeDtypeStruct((STATE, HEAD), F32)
    keep, send = call(
        attend_kernel,
        (state, state),
        (core,),
        (pos, kv, q, q_other, mine, theirs),
        "attend",
        cost=pl.CostEstimate(
            flops=8 * rows * keys * HEAD, bytes_accessed=keys * 512, transcendentals=rows * keys
        ),
    )
    got = lax.ppermute(send, "c", [(0, 1), (1, 0)])
    messages = call(
        merge_kernel,
        jax.ShapeDtypeStruct((4, MESSAGE, WIDTH), BF16),
        (core,),
        (keep, got),
        "merge",
        scratch=[pltpu.VMEM((4, MESSAGE, WIDTH), F32)],
    )

    got = []
    for k in range(4):
        pairs = []
        for at in range(16):
            h1, h0, l, c = (at >> 3) & 1, (at >> 2) & 1, (at >> 1) & 1, at & 1
            pairs.append((at, (((2 * h1 + c + k) % 4) * 2 + l) * 2 + h0))
        got.append(lax.ppermute(messages[k], ("zh", "zl", "c"), pairs))
    return call(
        place_kernel,
        (
            jax.ShapeDtypeStruct((4 * NEW, 2 * WIDTH), BF16),
            jax.ShapeDtypeStruct((2, 2, 2 * WIDTH), BF16),
        ),
        (core,),
        got,
        "place",
    )


def solution(mesh):
    fine = Mesh(mesh.devices.reshape(4, 4, 4, 2, 2), ALL)
    return jax.shard_map(
        shards,
        mesh=fine,
        in_specs=(
            P(ALL, None),
            P(ALL, None),
            P(ALL, None),
            P(),
            P(ALL, None),
            P(ALL, None),
            P(GRP, SEQ),
            P(SEQ, GRP),
            P(SEQ, GRP),
            P(SEQ, GRP),
            P(),
            P(),
        ),
        out_specs=(P(SEQ, GRP), P(SEQ, None, GRP)),
        check_vma=False,
    )
```

```python
import jax
import jax.numpy as jnp
import numpy as np
from jax import lax
from jax.experimental import pallas as pl
from jax.experimental.pallas import tpu as pltpu
from jax.sharding import Mesh, PartitionSpec as P

HEAD = 128
GROUP = 8
WIDTH = GROUP * HEAD
EXP2_SCALE = HEAD ** (-0.5) * 1.4426950408889634
HIDE = -1e30
ALL = ("zh", "x", "y", "zl", "c")
SEQ = ("zh", "x", "y")
GRP = ("zl", "c")
DEPTH = ("zh", "zl")
OLD, NEW = 32, 16
BOTH = OLD + NEW
TOKENS = 8 * NEW
BEAMS = 8
TILES = 11 * BEAMS
ACC = WIDTH + TOKENS
STATE = ACC + 32
MESSAGE = WIDTH + HEAD
VMEM = pltpu.CompilerParams(vmem_limit_bytes=56 * 1024 * 1024)
SMEM_SPEC = pl.BlockSpec(memory_space=pltpu.SMEM)
VMEM_SPEC = pl.BlockSpec(memory_space=pltpu.VMEM)
BF16, F32 = jnp.bfloat16, jnp.float32


def dot_nt(a, b):
    return lax.dot_general(a, b, (((1,), (1,)), ((), ())), preferred_element_type=F32)


def dot_nn(a, b):
    return lax.dot_general(a, b, (((1,), (0,)), ((), ())), preferred_element_type=F32)


def call(kernel, out_shape, scalars, args, name, cost=None, scratch=()):
    return pl.pallas_call(
        kernel,
        out_shape=out_shape,
        in_specs=[SMEM_SPEC] * len(scalars) + [VMEM_SPEC] * len(args),
        out_specs=jax.tree.map(lambda _: VMEM_SPEC, out_shape),
        scratch_shapes=list(scratch),
        cost_estimate=cost,
        compiler_params=VMEM,
        name=name,
    )(*scalars, *args)


def head_of(plane):
    return 4 * (plane & 1) + 2 * ((plane >> 1) & 1) + (plane >> 2)


def pack_kv_kernel(old_k, old_v, new_k, new_v, out):
    for plane in range(8):
        cols = slice(head_of(plane) * HEAD, (head_of(plane) + 1) * HEAD)
        out[plane, :OLD, :HEAD] = old_k[:, cols]
        out[plane, :OLD, HEAD:] = old_v[:, cols]
        out[plane, OLD:, :HEAD] = new_k[:, cols]
        out[plane, OLD:, HEAD:] = new_v[:, cols]


def pack_q_kernel(q, out):
    for plane in range(8):
        for pair in range(4):
            at = head_of(plane) * WIDTH + pair * 2 * HEAD
            out[plane, pair * NEW : (pair + 1) * NEW, :] = q[:, at : at + 2 * HEAD]


def hidden_kernel(owner, looked, out):
    rows = jnp.zeros((looked.shape[1], HEAD), F32)
    for part in range(4):
        rows = rows + jnp.where(owner[...] == part, looked[part].astype(F32), 0.0)
    rows = rows.astype(BF16)
    for part in range(4):
        out[part] = rows


def project_kernel(first, parent, beam_id, hidden, *refs):
    weights, (out, total, extra) = refs[:4], refs[4:]
    beams = extra.shape[0]
    pick = jnp.where(parent[...] == beam_id[...], 1.0, 0.0).astype(BF16)
    acc = acc_extra = 0.0
    for k in range(4):
        rows = hidden[first[0] ^ k]
        acc = acc + dot_nn(rows, weights[k][...])
        chosen = dot_nn(pick, rows[:beams]).astype(BF16)
        acc_extra = acc_extra + dot_nn(chosen, weights[k][:, 4 * HEAD :])
    total[...] = acc
    extra[...] = acc_extra
    for chip in range(16):
        for step in range(2):
            rows = slice(step * beams + chip * BEAMS, step * beams + (chip + 1) * BEAMS)
            for head in range(4):
                at = (step * 4 + head) * BEAMS
                out[chip, at : at + BEAMS, :] = total[rows, head * HEAD : (head + 1) * HEAD]
            at = (8 + step) * BEAMS
            out[chip, at : at + BEAMS, :] = total[rows, 4 * HEAD :]
        out[chip, 10 * BEAMS :, :] = extra[chip * BEAMS : (chip + 1) * BEAMS, :]


def sum_kernel(parts, out):
    terms = [parts[i] for i in range(parts.shape[0])]
    while len(terms) > 1:
        terms = [a + b for a, b in zip(terms[::2], terms[1::2])]
    out[...] = terms[0]


def attend_kernel(core, pos, kv, q_own, q_other, mine, theirs, keep, send):
    me = core[0]
    per_step = 4
    steps = kv.shape[0] // per_step
    place = core[1]

    def column(which):
        row = pos[pl.ds(which * 16 + place, 1), :].astype(F32)
        return jnp.transpose(jnp.broadcast_to(row, (TOKENS, HEAD)))[:, :1]

    qpos = (column(me), column(1 - me))
    halves = [jnp.where(me == 0, mine[...], theirs[...]), jnp.where(me == 0, theirs[...], mine[...])]
    queries = jnp.concatenate([h[: 8 * BEAMS] for h in halves], 0).astype(BF16)

    def query(block):
        if block == 2 * GROUP:
            return queries
        source = q_own if block < GROUP else q_other
        head = block % GROUP
        rows = slice((head // 2) * NEW, (head // 2 + 1) * NEW)
        lanes = slice((head % 2) * HEAD, (head % 2 + 1) * HEAD)
        return source[:, rows, lanes].reshape(TOKENS, HEAD)

    tiles = {}

    def load(step):
        part = slice(step * per_step, (step + 1) * per_step)
        wide = []
        for low, high in ((0, OLD), (OLD, BOTH)):
            count = per_step * 8 * (high - low)
            k = kv[part, :, low:high, :HEAD].reshape(count, HEAD)
            v = kv[part, :, low:high, HEAD:].reshape(count, HEAD)
            wide.append((k, jnp.concatenate([v, jnp.ones_like(v)], 1)))
        rows = [pos[pl.ds(me * 16 + step * per_step + i, 1), :] for i in range(per_step)]
        kpos = jnp.concatenate(rows, 1).astype(F32)
        bias = [jnp.where(kpos <= p, 0.0, HIDE) for p in qpos]
        tiles[step] = (wide, bias)

    def scores(step, block):
        if step not in tiles:
            load(step)
        wide, bias = tiles[step]
        q = query(block)
        s_old = dot_nt(q, wide[0][0])
        s_new = dot_nt(q, wide[1][0])
        if block < 2 * GROUP:
            s_new = s_new + bias[block // GROUP]
        return s_old, s_new

    def places(block):
        if block < GROUP:
            return keep, block
        if block < 2 * GROUP:
            return send, block - GROUP
        return keep, GROUP

    def absorb(step, block, pair):
        ref, slot = places(block)
        rows = slice(slot * TOKENS, (slot + 1) * TOKENS)
        peak = jnp.maximum(
            jnp.max(pair[0], axis=-1, keepdims=True), jnp.max(pair[1], axis=-1, keepdims=True)
        )
        if step > 0:
            top, total, acc = state[block]
            peak = jnp.maximum(top, peak)
            alpha = jnp.exp2((top - peak) * EXP2_SCALE)
        else:
            peak = jnp.broadcast_to(peak, (TOKENS, HEAD))
        mixed = 0.0
        for s, (_, v) in zip(pair, tiles[step][0]):
            w = jnp.exp2((s - peak[:, :1]) * EXP2_SCALE).astype(BF16)
            mixed = mixed + dot_nn(w, v)
        acc_new, total_new = mixed[:, :HEAD], mixed[:, HEAD:]
        if step > 0:
            acc_new = acc_new + acc[...] * alpha
            total_new = total_new + total[...] * alpha
        return peak, total_new, acc_new

    state = {}
    order = [(step, block) for step in range(steps) for block in range(2 * GROUP + 1)]
    ahead = scores(*order[0])
    for i, (step, block) in enumerate(order):
        now = ahead
        if i + 1 < len(order):
            ahead = scores(*order[i + 1])
        state[block] = absorb(step, block, now)

    top, total, acc = state[2 * GROUP]
    count = 4 * BEAMS
    pad = jnp.zeros((count - 3 * BEAMS, HEAD), F32)
    own_k = jnp.concatenate([halves[0][8 * BEAMS :], pad], 0).astype(BF16)
    own_v = jnp.concatenate([halves[1][8 * BEAMS :], pad], 0).astype(BF16)
    row = lax.broadcasted_iota(jnp.int32, (TOKENS, count), 0)
    key = lax.broadcasted_iota(jnp.int32, (TOKENS, count), 1)
    step = (row // (4 * BEAMS)) % 2
    beam = row % BEAMS
    slot = key // BEAMS
    first = jnp.logical_and(step == 0, slot == 0)
    second = jnp.logical_and(step == 1, jnp.logical_or(slot == 1, slot == 2))
    seen = jnp.logical_and(beam == key % BEAMS, jnp.logical_or(first, second))
    seen = jnp.logical_and(seen, beam // 4 == me)
    own = jnp.where(seen, dot_nt(queries, own_k), HIDE)
    peak = jnp.maximum(top, jnp.max(own, axis=-1, keepdims=True))
    alpha = jnp.exp2((top - peak) * EXP2_SCALE)
    w = jnp.exp2((own - peak[:, :1]) * EXP2_SCALE)
    total = total * alpha + jnp.sum(w, axis=-1, keepdims=True)
    acc = acc * alpha + dot_nn(w.astype(BF16), own_v)
    state[2 * GROUP] = (peak, total, acc)

    for block in range(2 * GROUP + 1):
        ref, slot = places(block)
        top, total, acc = state[block]
        rows = slice(slot * TOKENS, (slot + 1) * TOKENS)
        top, total = jnp.transpose(top)[:1], jnp.transpose(total)[:1]
        for target in (keep, send) if block == 2 * GROUP else (ref,):
            target[rows, :] = acc
            target[ACC + slot : ACC + slot + 1, :] = top
            target[ACC + 16 + slot : ACC + 17 + slot, :] = total


def merge_kernel(core, keep, got, *refs):
    out, message = refs[:4], refs[4]
    me, first = core[0], core[2]
    for zh in range(4):
        message[zh, NEW:, WIDTH:] = jnp.zeros((NEW, HEAD), F32)

    def spread(ref, row):
        return jnp.transpose(jnp.broadcast_to(ref[row : row + 1, :], (TOKENS, HEAD)))

    for slot in range(GROUP + 1):
        rows = slice(slot * TOKENS, (slot + 1) * TOKENS)
        top_a, top_b = spread(keep, ACC + slot), spread(got, ACC + slot)
        peak = jnp.maximum(top_a, top_b)
        a, b = jnp.exp2((top_a - peak) * EXP2_SCALE), jnp.exp2((top_b - peak) * EXP2_SCALE)
        total = spread(keep, ACC + 16 + slot) * a + spread(got, ACC + 16 + slot) * b
        mixed = (keep[rows, :] * a + got[rows, :] * b) / total
        if slot < GROUP:
            lanes = slice(slot * HEAD, (slot + 1) * HEAD)
            for zh in range(4):
                message[zh, :, lanes] = mixed[zh * 2 * NEW : (zh + 1) * 2 * NEW]
        else:
            for block in range(16):
                half, step, head = block // 8, (block // 4) % 2, block % 4
                at = step * GROUP + half * 4 + head
                tile = mixed[block * BEAMS : (block + 1) * BEAMS]
                tile = jnp.where(me == 0, tile[:4], tile[4:])
                for zh in range(4):
                    message[zh, at : at + 1, WIDTH:] = tile[zh : zh + 1]
    for k in range(4):
        out[k][...] = message[(first + k) % 4].astype(BF16)


def place_kernel(core, *refs):
    got, (stretch, decode) = refs[:4], refs[4:]
    zh = core[3]
    few = [jnp.zeros((NEW, HEAD), F32)] * 4
    for k in range(4):
        origin = (zh - k + 4) % 4
        lane = pl.multiple_of((origin // 2) * WIDTH, WIDTH)
        for low in range(2):
            row = pl.multiple_of(low * 2 * NEW + (origin % 2) * NEW, NEW)
            stretch[pl.ds(row, NEW), pl.ds(lane, WIDTH)] = got[k][
                low * NEW : (low + 1) * NEW, :WIDTH
            ]
        tail = got[k][:NEW, WIDTH:].astype(F32)
        few = [jnp.where(origin == i, tail, f) for i, f in enumerate(few)]
    for i in range(4):
        head, parity = i // 2, i % 2
        steps = [
            jnp.concatenate([few[i][s * GROUP + g : s * GROUP + g + 1] for g in range(GROUP)], 1)
            for s in range(2)
        ]
        decode[parity, :, head * WIDTH : (head + 1) * WIDTH] = jnp.concatenate(steps, 0).astype(BF16)


def shards(
    block_query_rows,
    block_key_rows,
    block_value_rows,
    stretch_pos,
    prompt_key_cache,
    prompt_value_cache,
    embed_table,
    query_weight,
    key_weight,
    value_weight,
    beam_tokens,
    parent_beam,
):
    zh, xi, yi, ci = (lax.axis_index(a) for a in ("zh", "x", "y", "c"))
    core = jnp.stack([ci, xi * 4 + yi, 2 * (zh // 2) + ci, zh]).astype(jnp.int32)

    kv = call(
        pack_kv_kernel,
        jax.ShapeDtypeStruct((8, BOTH, 2 * HEAD), BF16),
        (),
        (prompt_key_cache, prompt_value_cache, block_key_rows, block_value_rows),
        "pack_kv",
    )
    kv = lax.all_to_all(kv, DEPTH, split_axis=0, concat_axis=0, tiled=True)

    depth = query_weight.shape[0]
    q_cols = query_weight.shape[1] // 4
    parts = jnp.concatenate(
        [
            query_weight.reshape(depth, 2, 2, q_cols),
            jnp.stack([key_weight.reshape(depth, 2, HEAD), value_weight.reshape(depth, 2, HEAD)], 2),
        ],
        -1,
    )
    parts = jnp.transpose(parts, (1, 2, 0, 3)).reshape(4, depth, q_cols + HEAD)
    mine = [lax.dynamic_index_in_dim(parts, zh ^ k, 0, keepdims=False) for k in range(4)]
    kv, mine = lax.optimization_barrier((kv, mine))
    weights = []
    for k in range(4):
        pairs = []
        for at in range(8):
            h, c = at // 2, at % 2
            to = h ^ k
            pairs.append((at, (2 * (to // 2) + c) * 2 + to % 2))
        weights.append(lax.ppermute(mine[k], ("zh", "c"), pairs))

    kv = lax.all_gather(kv.reshape(8 * BOTH, 2 * HEAD), ("x", "y"), axis=0, tiled=True)
    kv = kv.reshape(16, 8, BOTH, 2 * HEAD)

    pos = jnp.transpose(stretch_pos.reshape(4, 4, 4, 2, 2, NEW), (4, 1, 2, 0, 3, 5))
    pos = pos.reshape(32, TOKENS)

    vocab_rows = embed_table.shape[0]
    beams = beam_tokens.shape[0]
    ids = jnp.transpose(beam_tokens.reshape(4, 4, 4, 2, 2), (4, 2, 1, 3, 0)).reshape(-1)
    looked = embed_table.at[ids % vocab_rows].get(mode="promise_in_bounds")
    looked = lax.all_to_all(
        jnp.broadcast_to(looked, (4,) + looked.shape), GRP, split_axis=0, concat_axis=0, tiled=True
    )
    looked, weights = lax.optimization_barrier((looked, weights))
    hidden = call(
        hidden_kernel,
        jax.ShapeDtypeStruct((4, 2 * beams, HEAD), BF16),
        (),
        ((ids // vocab_rows)[:, None], looked),
        "hidden",
    )
    hidden = lax.all_to_all(hidden, "zh", split_axis=0, concat_axis=0, tiled=True)

    q = call(
        pack_q_kernel,
        jax.ShapeDtypeStruct((8, 4 * NEW, 2 * HEAD), BF16),
        (),
        (block_query_rows,),
        "pack_q",
    )
    hidden, q = lax.optimization_barrier((hidden, q))
    q = lax.all_to_all(q, DEPTH, split_axis=0, concat_axis=0, tiled=True)
    q_other = lax.ppermute(q, "c", [(0, 1), (1, 0)])

    beam_id = np.arange(beams, dtype=np.int32).reshape(4, 4, 4, 2).transpose(2, 1, 3, 0)
    parent = jnp.transpose(parent_beam.reshape(4, 4, 4, 2), (2, 1, 3, 0))
    part = call(
        project_kernel,
        jax.ShapeDtypeStruct((16, TILES, HEAD), F32),
        (core[2:3],),
        (parent.reshape(-1, 1), beam_id.reshape(1, -1), hidden, *weights),
        "project",
        scratch=[
            pltpu.VMEM((2 * beams, q_cols + HEAD), F32),
            pltpu.VMEM((beams, HEAD), F32),
        ],
    )
    part = lax.all_to_all(part, ("y", "x"), split_axis=0, concat_axis=0, tiled=True)
    mine = call(sum_kernel, jax.ShapeDtypeStruct((TILES, HEAD), F32), (), (part,), "sum")
    theirs = lax.ppermute(mine, "c", [(0, 1), (1, 0)])

    rows = (2 * GROUP + 1) * TOKENS
    keys = 16 * 8 * BOTH
    state = jax.ShapeDtypeStruct((STATE, HEAD), F32)
    keep, send = call(
        attend_kernel,
        (state, state),
        (core,),
        (pos, kv, q, q_other, mine, theirs),
        "attend",
        cost=pl.CostEstimate(
            flops=8 * rows * keys * HEAD, bytes_accessed=keys * 512, transcendentals=rows * keys
        ),
    )
    got = lax.ppermute(send, "c", [(0, 1), (1, 0)])
    messages = call(
        merge_kernel,
        [jax.ShapeDtypeStruct((2 * NEW, MESSAGE), BF16)] * 4,
        (core,),
        (keep, got),
        "merge",
        scratch=[pltpu.VMEM((4, 2 * NEW, MESSAGE), F32)],
    )

    got = []
    for k in range(4):
        pairs = []
        for at in range(16):
            h1, h0, l, c = (at >> 3) & 1, (at >> 2) & 1, (at >> 1) & 1, at & 1
            pairs.append((at, (((2 * h1 + c + k) % 4) * 2 + l) * 2 + h0))
        got.append(lax.ppermute(messages[k], ("zh", "zl", "c"), pairs))
    return call(
        place_kernel,
        (
            jax.ShapeDtypeStruct((4 * NEW, 2 * WIDTH), BF16),
            jax.ShapeDtypeStruct((2, 2, 2 * WIDTH), BF16),
        ),
        (core,),
        got,
        "place",
    )


def solution(mesh):
    fine = Mesh(mesh.devices.reshape(4, 4, 4, 2, 2), ALL)
    return jax.shard_map(
        shards,
        mesh=fine,
        in_specs=(
            P(ALL, None),
            P(ALL, None),
            P(ALL, None),
            P(),
            P(ALL, None),
            P(ALL, None),
            P(GRP, SEQ),
            P(SEQ, GRP),
            P(SEQ, GRP),
            P(SEQ, GRP),
            P(),
            P(),
        ),
        out_specs=(P(SEQ, GRP), P(SEQ, None, GRP)),
        check_vma=False,
    )
```

```python
import jax
import jax.numpy as jnp
import numpy as np
from jax import lax
from jax.experimental import pallas as pl
from jax.experimental.pallas import tpu as pltpu
from jax.sharding import Mesh, PartitionSpec as P

HEAD = 128
GROUP = 8
WIDTH = GROUP * HEAD
EXP2_SCALE = HEAD ** (-0.5) * 1.4426950408889634
HIDE = -1e30
ALL = ("zh", "x", "y", "zl", "c")
SEQ = ("zh", "x", "y")
GRP = ("zl", "c")
DEPTH = ("zh", "zl")
OLD, NEW = 32, 16
BOTH = OLD + NEW
TOKENS = 8 * NEW
BEAMS = 8
TILES = 11 * BEAMS
SHIFTS = (1, 3, 2)
MESSAGE = WIDTH + HEAD
VMEM = pltpu.CompilerParams(vmem_limit_bytes=56 * 1024 * 1024)
SMEM_SPEC = pl.BlockSpec(memory_space=pltpu.SMEM)
VMEM_SPEC = pl.BlockSpec(memory_space=pltpu.VMEM)
BF16, F32 = jnp.bfloat16, jnp.float32


def dot_nt(a, b):
    return lax.dot_general(a, b, (((1,), (1,)), ((), ())), preferred_element_type=F32)


def dot_nn(a, b):
    return lax.dot_general(a, b, (((1,), (0,)), ((), ())), preferred_element_type=F32)


def call(kernel, out_shape, scalars, args, name, cost=None, scratch=()):
    return pl.pallas_call(
        kernel,
        out_shape=out_shape,
        in_specs=[SMEM_SPEC] * len(scalars) + [VMEM_SPEC] * len(args),
        out_specs=jax.tree.map(lambda _: VMEM_SPEC, out_shape),
        scratch_shapes=list(scratch),
        cost_estimate=cost,
        compiler_params=VMEM,
        name=name,
    )(*scalars, *args)


def head_of(plane):
    return 4 * (plane & 1) + 2 * ((plane >> 1) & 1) + (plane >> 2)


def pack_kernel(old_k, old_v, new_k, new_v, q, out):
    for plane in range(8):
        head = head_of(plane)
        cols = slice(head * HEAD, (head + 1) * HEAD)
        out[plane, :OLD, :HEAD] = old_k[:, cols]
        out[plane, :OLD, HEAD:] = old_v[:, cols]
        out[plane, OLD:BOTH, :HEAD] = new_k[:, cols]
        out[plane, OLD:BOTH, HEAD:] = new_v[:, cols]
        for pair in range(4):
            at = head * WIDTH + pair * 2 * HEAD
            out[plane, BOTH + pair * NEW : BOTH + (pair + 1) * NEW, :] = q[:, at : at + 2 * HEAD]


def hidden_kernel(owner, looked, out):
    rows = jnp.zeros((looked.shape[1], HEAD), F32)
    for part in range(4):
        rows = rows + jnp.where(owner[...] == part, looked[part].astype(F32), 0.0)
    rows = rows.astype(BF16)
    for part in range(4):
        out[part] = rows


def project_kernel(first, parent, beam_id, hidden, *refs):
    weights, (out, total, extra) = refs[:4], refs[4:]
    beams = extra.shape[0]
    pick = jnp.where(parent[...] == beam_id[...], 1.0, 0.0).astype(BF16)
    acc = acc_extra = 0.0
    for k in range(4):
        rows = hidden[first[0] ^ k]
        acc = acc + dot_nn(rows, weights[k][...])
        chosen = dot_nn(pick, rows[:beams]).astype(BF16)
        acc_extra = acc_extra + dot_nn(chosen, weights[k][:, 4 * HEAD :])
    total[...] = acc
    extra[...] = acc_extra
    for chip in range(16):
        for step in range(2):
            rows = slice(step * beams + chip * BEAMS, step * beams + (chip + 1) * BEAMS)
            for head in range(4):
                at = (step * 4 + head) * BEAMS
                out[chip, at : at + BEAMS, :] = total[rows, head * HEAD : (head + 1) * HEAD]
            at = (8 + step) * BEAMS
            out[chip, at : at + BEAMS, :] = total[rows, 4 * HEAD :]
        out[chip, 10 * BEAMS :, :] = extra[chip * BEAMS : (chip + 1) * BEAMS, :]


def sum_kernel(parts, out):
    terms = [parts[i] for i in range(parts.shape[0])]
    while len(terms) > 1:
        terms = [a + b for a, b in zip(terms[::2], terms[1::2])]
    out[...] = terms[0]


def spread(ref, row):
    return jnp.transpose(jnp.broadcast_to(ref[row : row + 1, :], (TOKENS, HEAD)))


def load_lines(pair):
    wide = []
    for low, high in ((0, OLD), (OLD, BOTH)):
        count = 16 * (high - low)
        k = jnp.concatenate([r[:, :, low:high, :HEAD].reshape(count, HEAD) for r in pair], 0)
        v = jnp.concatenate([r[:, :, low:high, HEAD:].reshape(count, HEAD) for r in pair], 0)
        wide.append((k, jnp.concatenate([v, jnp.ones_like(v)], 1)))
    return wide


def absorb(state, tiles, wide):
    peak = jnp.maximum(
        jnp.max(tiles[0], axis=-1, keepdims=True), jnp.max(tiles[1], axis=-1, keepdims=True)
    )
    if state is None:
        peak = jnp.broadcast_to(peak, (TOKENS, HEAD))
    else:
        top, total, acc = state
        peak = jnp.maximum(top, peak)
        alpha = jnp.exp2((top - peak) * EXP2_SCALE)
    mixed = 0.0
    for s, (_, v) in zip(tiles, wide):
        w = jnp.exp2((s - peak[:, :1]) * EXP2_SCALE).astype(BF16)
        mixed = mixed + dot_nn(w, v)
    if state is None:
        return peak, mixed[:, HEAD:], mixed[:, :HEAD]
    return peak, mixed[:, HEAD:] + total * alpha, mixed[:, :HEAD] + acc * alpha


def put_state(ref, slot, slots, state):
    top, total, acc = state
    ref[slot * TOKENS : (slot + 1) * TOKENS, :] = acc
    at = slots * TOKENS + slot
    ref[at : at + 1, :] = jnp.transpose(top)[:1]
    at = at + slots
    ref[at : at + 1, :] = jnp.transpose(total)[:1]


def get_state(ref, slot, slots):
    at = slots * TOKENS + slot
    return spread(ref, at), spread(ref, at + slots), ref[slot * TOKENS : (slot + 1) * TOKENS, :]


def attend_kernel(shifts, resumed, core, pos, lines, own, other, *refs):
    if resumed:
        states, refs = refs[:2], refs[2:]
    kv, (keep, send) = refs[:-2], refs[-2:]
    me, place, xi, yi = core[0], core[1], core[4], core[5]

    def column(which):
        row = pos[pl.ds(which * 16 + place, 1), :].astype(F32)
        return jnp.transpose(jnp.broadcast_to(row, (TOKENS, HEAD)))[:, :1]

    qpos = (column(me), column(1 - me))
    loaded = {}

    def scores(step, block):
        if step not in loaded:
            back = 4 - shifts[step]
            a = lines[pl.ds(me * 4 + (yi + back) % 4, 1), :]
            b = lines[pl.ds(8 + me * 4 + (xi + back) % 4, 1), :]
            kpos = jnp.concatenate([a, b], 1).astype(F32)
            bias = [jnp.where(kpos <= p, 0.0, HIDE) for p in qpos]
            loaded[step] = (load_lines(kv[2 * step : 2 * step + 2]), bias)
        wide, bias = loaded[step]
        head = block % GROUP
        lanes = slice((head % 2) * HEAD, (head % 2 + 1) * HEAD)
        if block < GROUP:
            at = BOTH + (head // 2) * NEW
            q = own[:, at : at + NEW, lanes].reshape(TOKENS, HEAD)
        else:
            at = (head // 2) * NEW
            q = other[:, at : at + NEW, lanes].reshape(TOKENS, HEAD)
        return dot_nt(q, wide[0][0]), dot_nt(q, wide[1][0]) + bias[block // GROUP]

    state = {}
    order = [(step, block) for step in range(len(shifts)) for block in range(2 * GROUP)]
    ahead = scores(*order[0])
    for i, (step, block) in enumerate(order):
        now = ahead
        if i + 1 < len(order):
            ahead = scores(*order[i + 1])
        if step == 0:
            state[block] = get_state(states[block // GROUP], block % GROUP, GROUP) if resumed else None
        state[block] = absorb(state[block], now, loaded[step][0])
        if step == len(shifts) - 1:
            put_state((keep, send)[block // GROUP], block % GROUP, GROUP, state[block])


def decode_kernel(core, mine, theirs, *refs):
    kv, out = refs[:-1], refs[-1]
    me = core[0]
    halves = [jnp.where(me == 0, mine[...], theirs[...]), jnp.where(me == 0, theirs[...], mine[...])]
    queries = jnp.concatenate([h[: 8 * BEAMS] for h in halves], 0).astype(BF16)
    state = None
    steps = len(kv) // 2
    wide = load_lines(kv[:2])
    ahead = [dot_nt(queries, k) for k, _ in wide]
    for step in range(steps):
        now, now_wide = ahead, wide
        if step + 1 < steps:
            wide = load_lines(kv[2 * step + 2 : 2 * step + 4])
            ahead = [dot_nt(queries, k) for k, _ in wide]
        state = absorb(state, now, now_wide)

    top, total, acc = state
    count = 4 * BEAMS
    pad = jnp.zeros((count - 3 * BEAMS, HEAD), F32)
    own_k = jnp.concatenate([halves[0][8 * BEAMS :], pad], 0).astype(BF16)
    own_v = jnp.concatenate([halves[1][8 * BEAMS :], pad], 0).astype(BF16)
    row = lax.broadcasted_iota(jnp.int32, (TOKENS, count), 0)
    key = lax.broadcasted_iota(jnp.int32, (TOKENS, count), 1)
    step = (row // (4 * BEAMS)) % 2
    beam = row % BEAMS
    slot = key // BEAMS
    first = jnp.logical_and(step == 0, slot == 0)
    second = jnp.logical_and(step == 1, jnp.logical_or(slot == 1, slot == 2))
    seen = jnp.logical_and(beam == key % BEAMS, jnp.logical_or(first, second))
    seen = jnp.logical_and(seen, beam // 4 == me)
    own = jnp.where(seen, dot_nt(queries, own_k), HIDE)
    peak = jnp.maximum(top, jnp.max(own, axis=-1, keepdims=True))
    alpha = jnp.exp2((top - peak) * EXP2_SCALE)
    w = jnp.exp2((own - peak[:, :1]) * EXP2_SCALE)
    total = total * alpha + jnp.sum(w, axis=-1, keepdims=True)
    acc = acc * alpha + dot_nn(w.astype(BF16), own_v)
    put_state(out, 0, 1, (peak, total, acc))


def merge_kernel(core, keep, got, beams_keep, beams_got, *refs):
    out, message = refs[:4], refs[4]
    me, first = core[0], core[2]
    for zh in range(4):
        message[zh, NEW:, WIDTH:] = jnp.zeros((NEW, HEAD), F32)
    for slot in range(GROUP + 1):
        if slot < GROUP:
            parts = [get_state(ref, slot, GROUP) for ref in (keep, got)]
        else:
            parts = [get_state(ref, 0, 1) for ref in (beams_keep, beams_got)]
        peak = jnp.maximum(parts[0][0], parts[1][0])
        a, b = [jnp.exp2((p[0] - peak) * EXP2_SCALE) for p in parts]
        total = parts[0][1] * a + parts[1][1] * b
        mixed = (parts[0][2] * a + parts[1][2] * b) / total
        if slot < GROUP:
            lanes = slice(slot * HEAD, (slot + 1) * HEAD)
            for zh in range(4):
                message[zh, :, lanes] = mixed[zh * 2 * NEW : (zh + 1) * 2 * NEW]
        else:
            for block in range(16):
                half, step, head = block // 8, (block // 4) % 2, block % 4
                at = step * GROUP + half * 4 + head
                tile = mixed[block * BEAMS : (block + 1) * BEAMS]
                tile = jnp.where(me == 0, tile[:4], tile[4:])
                for zh in range(4):
                    message[zh, at : at + 1, WIDTH:] = tile[zh : zh + 1]
    for k in range(4):
        out[k][...] = message[(first + k) % 4].astype(BF16)


def place_kernel(core, *refs):
    got, (stretch, decode) = refs[:4], refs[4:]
    zh = core[3]
    few = [jnp.zeros((NEW, HEAD), F32)] * 4
    for k in range(4):
        origin = (zh - k + 4) % 4
        lane = pl.multiple_of((origin // 2) * WIDTH, WIDTH)
        for low in range(2):
            row = pl.multiple_of(low * 2 * NEW + (origin % 2) * NEW, NEW)
            stretch[pl.ds(row, NEW), pl.ds(lane, WIDTH)] = got[k][
                low * NEW : (low + 1) * NEW, :WIDTH
            ]
        tail = got[k][:NEW, WIDTH:].astype(F32)
        few = [jnp.where(origin == i, tail, f) for i, f in enumerate(few)]
    for i in range(4):
        head, parity = i // 2, i % 2
        steps = [
            jnp.concatenate([few[i][s * GROUP + g : s * GROUP + g + 1] for g in range(GROUP)], 1)
            for s in range(2)
        ]
        decode[parity, :, head * WIDTH : (head + 1) * WIDTH] = jnp.concatenate(steps, 0).astype(BF16)


def shards(
    block_query_rows,
    block_key_rows,
    block_value_rows,
    stretch_pos,
    prompt_key_cache,
    prompt_value_cache,
    embed_table,
    query_weight,
    key_weight,
    value_weight,
    beam_tokens,
    parent_beam,
):
    zh, xi, yi, ci = (lax.axis_index(a) for a in ("zh", "x", "y", "c"))
    core = jnp.stack([ci, xi * 4 + yi, 2 * (zh // 2) + ci, zh, xi, yi]).astype(jnp.int32)

    packed = call(
        pack_kernel,
        jax.ShapeDtypeStruct((8, BOTH + 4 * NEW, 2 * HEAD), BF16),
        (),
        (prompt_key_cache, prompt_value_cache, block_key_rows, block_value_rows, block_query_rows),
        "pack",
    )
    packed = lax.all_to_all(packed, DEPTH, split_axis=0, concat_axis=0, tiled=True)

    depth = query_weight.shape[0]
    q_cols = query_weight.shape[1] // 4
    parts = jnp.concatenate(
        [
            query_weight.reshape(depth, 2, 2, q_cols),
            jnp.stack([key_weight.reshape(depth, 2, HEAD), value_weight.reshape(depth, 2, HEAD)], 2),
        ],
        -1,
    )
    parts = jnp.transpose(parts, (1, 2, 0, 3)).reshape(4, depth, q_cols + HEAD)
    mine = [lax.dynamic_index_in_dim(parts, zh ^ k, 0, keepdims=False) for k in range(4)]
    packed, mine = lax.optimization_barrier((packed, mine))
    weights = []
    for k in range(4):
        pairs = []
        for at in range(8):
            h, c = at // 2, at % 2
            to = h ^ k
            pairs.append((at, (2 * (to // 2) + c) * 2 + to % 2))
        weights.append(lax.ppermute(mine[k], ("zh", "c"), pairs))

    line_a = jnp.broadcast_to(packed[:4, :BOTH], (4, 4, BOTH, 2 * HEAD))
    line_b = jnp.broadcast_to(packed[4:, :BOTH], (4, 4, BOTH, 2 * HEAD))
    line_a = lax.all_to_all(line_a, "x", split_axis=0, concat_axis=0, tiled=True)
    line_b = lax.all_to_all(line_b, "y", split_axis=0, concat_axis=0, tiled=True)
    lines = [line_a, line_b]
    for k in SHIFTS:
        pairs = [(i, (i + k) % 4) for i in range(4)]
        lines.append(lax.ppermute(line_a, "y", pairs))
        lines.append(lax.ppermute(line_b, "x", pairs))
    q_other = lax.ppermute(packed[:, BOTH:], "c", [(0, 1), (1, 0)])

    pos = jnp.transpose(stretch_pos.reshape(4, 4, 4, 2, 2, NEW), (4, 1, 2, 0, 3, 5))
    halves = pos.reshape(2, 4, 4, 2, TOKENS // 2)
    pos = pos.reshape(32, TOKENS)
    line_pos = jnp.stack(
        [
            jnp.transpose(halves[:, :, :, 0], (0, 2, 1, 3)).reshape(8, 2 * TOKENS),
            halves[:, :, :, 1].reshape(8, 2 * TOKENS),
        ]
    ).reshape(16, 2 * TOKENS)

    vocab_rows = embed_table.shape[0]
    beams = beam_tokens.shape[0]
    ids = jnp.transpose(beam_tokens.reshape(4, 4, 4, 2, 2), (4, 2, 1, 3, 0)).reshape(-1)
    looked = embed_table.at[ids % vocab_rows].get(mode="promise_in_bounds")
    looked = lax.all_to_all(
        jnp.broadcast_to(looked, (4,) + looked.shape), GRP, split_axis=0, concat_axis=0, tiled=True
    )
    looked, weights = lax.optimization_barrier((looked, weights))
    hidden = call(
        hidden_kernel,
        jax.ShapeDtypeStruct((4, 2 * beams, HEAD), BF16),
        (),
        ((ids // vocab_rows)[:, None], looked),
        "hidden",
    )
    hidden = lax.all_to_all(hidden, "zh", split_axis=0, concat_axis=0, tiled=True)

    beam_id = np.arange(beams, dtype=np.int32).reshape(4, 4, 4, 2).transpose(2, 1, 3, 0)
    parent = jnp.transpose(parent_beam.reshape(4, 4, 4, 2), (2, 1, 3, 0))
    part = call(
        project_kernel,
        jax.ShapeDtypeStruct((16, TILES, HEAD), F32),
        (core[2:3],),
        (parent.reshape(-1, 1), beam_id.reshape(1, -1), hidden, *weights),
        "project",
        scratch=[
            pltpu.VMEM((2 * beams, q_cols + HEAD), F32),
            pltpu.VMEM((beams, HEAD), F32),
        ],
    )
    part = lax.all_to_all(part, ("y", "x"), split_axis=0, concat_axis=0, tiled=True)
    mine = call(sum_kernel, jax.ShapeDtypeStruct((TILES, HEAD), F32), (), (part,), "sum")
    theirs = lax.ppermute(mine, "c", [(0, 1), (1, 0)])

    def attend(shifts, carry, pieces, name):
        work = 2 * GROUP * TOKENS * len(shifts) * 32 * BOTH
        state = jax.ShapeDtypeStruct((GROUP * (TOKENS + 2), HEAD), F32)
        return call(
            lambda *refs: attend_kernel(shifts, bool(carry), *refs),
            (state, state),
            (core,),
            (pos, line_pos, packed, q_other, *carry, *pieces),
            name,
            cost=pl.CostEstimate(
                flops=8 * work * HEAD, bytes_accessed=work // 4, transcendentals=work
            ),
        )

    carry = attend((0,), (), lines[:2], "attend_near")
    keep, send = attend(SHIFTS, carry, lines[2:], "attend_far")
    got = lax.ppermute(send, "c", [(0, 1), (1, 0)])
    beams_keep = call(
        decode_kernel,
        jax.ShapeDtypeStruct((TOKENS + 8, HEAD), F32),
        (core,),
        (mine, theirs, *lines),
        "decode",
        cost=pl.CostEstimate(
            flops=8 * TOKENS * 128 * BOTH * HEAD,
            bytes_accessed=512 * 128 * BOTH,
            transcendentals=TOKENS * 128 * BOTH,
        ),
    )
    beams_got = lax.ppermute(beams_keep, "c", [(0, 1), (1, 0)])
    messages = call(
        merge_kernel,
        [jax.ShapeDtypeStruct((2 * NEW, MESSAGE), BF16)] * 4,
        (core,),
        (keep, got, beams_keep, beams_got),
        "merge",
        scratch=[pltpu.VMEM((4, 2 * NEW, MESSAGE), F32)],
    )

    got = []
    for k in range(4):
        pairs = []
        for at in range(16):
            h1, h0, l, c = (at >> 3) & 1, (at >> 2) & 1, (at >> 1) & 1, at & 1
            pairs.append((at, (((2 * h1 + c + k) % 4) * 2 + l) * 2 + h0))
        got.append(lax.ppermute(messages[k], ("zh", "zl", "c"), pairs))
    return call(
        place_kernel,
        (
            jax.ShapeDtypeStruct((4 * NEW, 2 * WIDTH), BF16),
            jax.ShapeDtypeStruct((2, 2, 2 * WIDTH), BF16),
        ),
        (core,),
        got,
        "place",
    )


def solution(mesh):
    fine = Mesh(mesh.devices.reshape(4, 4, 4, 2, 2), ALL)
    return jax.shard_map(
        shards,
        mesh=fine,
        in_specs=(
            P(ALL, None),
            P(ALL, None),
            P(ALL, None),
            P(),
            P(ALL, None),
            P(ALL, None),
            P(GRP, SEQ),
            P(SEQ, GRP),
            P(SEQ, GRP),
            P(SEQ, GRP),
            P(),
            P(),
        ),
        out_specs=(P(SEQ, GRP), P(SEQ, None, GRP)),
        check_vma=False,
    )
```

```python
import jax
import jax.numpy as jnp
import numpy as np
from jax import lax
from jax.experimental import pallas as pl
from jax.experimental.pallas import tpu as pltpu
from jax.sharding import Mesh, PartitionSpec as P

HEAD = 128
GROUP = 8
WIDTH = GROUP * HEAD
EXP2_SCALE = HEAD ** (-0.5) * 1.4426950408889634
HIDE = -1e30
ALL = ("zh", "x", "y", "zl", "c")
SEQ = ("zh", "x", "y")
GRP = ("zl", "c")
DEPTH = ("zh", "zl")
OLD, NEW = 32, 16
BOTH = OLD + NEW
TOKENS = 8 * NEW
BEAMS = 8
TILES = 11 * BEAMS
MESSAGE = WIDTH + HEAD
VMEM = pltpu.CompilerParams(vmem_limit_bytes=56 * 1024 * 1024)
SMEM_SPEC = pl.BlockSpec(memory_space=pltpu.SMEM)
VMEM_SPEC = pl.BlockSpec(memory_space=pltpu.VMEM)
BF16, F32 = jnp.bfloat16, jnp.float32


def dot_nt(a, b):
    return lax.dot_general(a, b, (((1,), (1,)), ((), ())), preferred_element_type=F32)


def dot_nn(a, b):
    return lax.dot_general(a, b, (((1,), (0,)), ((), ())), preferred_element_type=F32)


def call(kernel, out_shape, scalars, args, name, cost=None, scratch=()):
    return pl.pallas_call(
        kernel,
        out_shape=out_shape,
        in_specs=[SMEM_SPEC] * len(scalars) + [VMEM_SPEC] * len(args),
        out_specs=jax.tree.map(lambda _: VMEM_SPEC, out_shape),
        scratch_shapes=list(scratch),
        cost_estimate=cost,
        compiler_params=VMEM,
        name=name,
    )(*scalars, *args)


def head_of(plane):
    return 4 * (plane & 1) + 2 * ((plane >> 1) & 1) + (plane >> 2)


def pack_kernel(old_k, old_v, new_k, new_v, q, out):
    for plane in range(8):
        head = head_of(plane)
        cols = slice(head * HEAD, (head + 1) * HEAD)
        out[plane, :OLD, :HEAD] = old_k[:, cols]
        out[plane, :OLD, HEAD:] = old_v[:, cols]
        out[plane, OLD:BOTH, :HEAD] = new_k[:, cols]
        out[plane, OLD:BOTH, HEAD:] = new_v[:, cols]
        for pair in range(4):
            at = head * WIDTH + pair * 2 * HEAD
            out[plane, BOTH + pair * NEW : BOTH + (pair + 1) * NEW, :] = q[:, at : at + 2 * HEAD]


def hidden_kernel(owner, looked, out):
    rows = jnp.zeros((looked.shape[1], HEAD), F32)
    for part in range(4):
        rows = rows + jnp.where(owner[...] == part, looked[part].astype(F32), 0.0)
    rows = rows.astype(BF16)
    for part in range(4):
        out[part] = rows


def project_kernel(parent, beam_id, hidden, weights, out, total, extra):
    beams = extra.shape[0]
    pick = jnp.where(parent[...] == beam_id[...], 1.0, 0.0).astype(BF16)
    acc = acc_extra = 0.0
    for k in range(4):
        rows = hidden[k]
        acc = acc + dot_nn(rows, weights[k])
        chosen = dot_nn(pick, rows[:beams]).astype(BF16)
        acc_extra = acc_extra + dot_nn(chosen, weights[k, :, 4 * HEAD :])
    total[...] = acc
    extra[...] = acc_extra
    for chip in range(16):
        for step in range(2):
            rows = slice(step * beams + chip * BEAMS, step * beams + (chip + 1) * BEAMS)
            for head in range(4):
                at = (step * 4 + head) * BEAMS
                out[chip, at : at + BEAMS, :] = total[rows, head * HEAD : (head + 1) * HEAD]
            at = (8 + step) * BEAMS
            out[chip, at : at + BEAMS, :] = total[rows, 4 * HEAD :]
        out[chip, 10 * BEAMS :, :] = extra[chip * BEAMS : (chip + 1) * BEAMS, :]


def sum_kernel(parts, out):
    terms = [parts[i] for i in range(parts.shape[0])]
    while len(terms) > 1:
        terms = [a + b for a, b in zip(terms[::2], terms[1::2])]
    out[...] = terms[0]


def spread(ref, row):
    return jnp.transpose(jnp.broadcast_to(ref[row : row + 1, :], (TOKENS, HEAD)))


def load_lines(pair):
    wide = []
    for low, high in ((0, OLD), (OLD, BOTH)):
        count = 16 * (high - low)
        k = jnp.concatenate([r[:, :, low:high, :HEAD].reshape(count, HEAD) for r in pair], 0)
        v = jnp.concatenate([r[:, :, low:high, HEAD:].reshape(count, HEAD) for r in pair], 0)
        wide.append((k, jnp.concatenate([v, jnp.ones_like(v)], 1)))
    return wide


def absorb(state, tiles, wide):
    peak = jnp.maximum(
        jnp.max(tiles[0], axis=-1, keepdims=True), jnp.max(tiles[1], axis=-1, keepdims=True)
    )
    if state is None:
        peak = jnp.broadcast_to(peak, (TOKENS, HEAD))
    else:
        top, total, acc = state
        peak = jnp.maximum(top, peak)
        alpha = jnp.exp2((top - peak) * EXP2_SCALE)
    mixed = 0.0
    for s, (_, v) in zip(tiles, wide):
        w = jnp.exp2((s - peak[:, :1]) * EXP2_SCALE).astype(BF16)
        mixed = mixed + dot_nn(w, v)
    if state is None:
        return peak, mixed[:, HEAD:], mixed[:, :HEAD]
    return peak, mixed[:, HEAD:] + total * alpha, mixed[:, :HEAD] + acc * alpha


def put_state(ref, slot, slots, state):
    top, total, acc = state
    ref[slot * TOKENS : (slot + 1) * TOKENS, :] = acc
    at = slots * TOKENS + slot
    ref[at : at + 1, :] = jnp.transpose(top)[:1]
    at = at + slots
    ref[at : at + 1, :] = jnp.transpose(total)[:1]


def get_state(ref, slot, slots):
    at = slots * TOKENS + slot
    return spread(ref, at), spread(ref, at + slots), ref[slot * TOKENS : (slot + 1) * TOKENS, :]


def attend_kernel(starts, resumed, core, pos, lines, own, other, *refs):
    if resumed:
        states, refs = refs[:2], refs[2:]
    kv, (keep, send) = refs[:-2], refs[-2:]
    me, place = core[0], core[1]

    def column(which):
        row = pos[pl.ds(which * 16 + place, 1), :].astype(F32)
        return jnp.transpose(jnp.broadcast_to(row, (TOKENS, HEAD)))[:, :1]

    qpos = (column(me), column(1 - me))
    loaded = {}

    def scores(step, block):
        if step not in loaded:
            first, part, line = starts[step]
            kpos = jnp.concatenate([lines[line : line + 1], lines[4 + line : 5 + line]], 1)
            kpos = kpos.astype(F32)
            bias = [jnp.where(kpos <= p, 0.0, HIDE) for p in qpos]
            pair = [r.at[4 * part : 4 * part + 4] for r in kv[first : first + 2]]
            loaded[step] = (load_lines(pair), bias)
        wide, bias = loaded[step]
        head = block % GROUP
        lanes = slice((head % 2) * HEAD, (head % 2 + 1) * HEAD)
        if block < GROUP:
            at = BOTH + (head // 2) * NEW
            q = own[:, at : at + NEW, lanes].reshape(TOKENS, HEAD)
        else:
            at = (head // 2) * NEW
            q = other[:, at : at + NEW, lanes].reshape(TOKENS, HEAD)
        return dot_nt(q, wide[0][0]), dot_nt(q, wide[1][0]) + bias[block // GROUP]

    state = {}
    order = [(step, block) for step in range(len(starts)) for block in range(2 * GROUP)]
    ahead = scores(*order[0])
    for i, (step, block) in enumerate(order):
        now = ahead
        if i + 1 < len(order):
            ahead = scores(*order[i + 1])
        if step == 0:
            state[block] = get_state(states[block // GROUP], block % GROUP, GROUP) if resumed else None
        state[block] = absorb(state[block], now, loaded[step][0])
        if step == len(starts) - 1:
            put_state((keep, send)[block // GROUP], block % GROUP, GROUP, state[block])


def decode_kernel(core, mine, theirs, *refs):
    kv, out = refs[:-1], refs[-1]
    me = core[0]
    halves = [jnp.where(me == 0, mine[...], theirs[...]), jnp.where(me == 0, theirs[...], mine[...])]
    queries = jnp.concatenate([h[: 8 * BEAMS] for h in halves], 0).astype(BF16)
    state = None
    pairs = []
    for i in range(0, len(kv), 2):
        for part in range(kv[i].shape[0] // 4):
            pairs.append([r.at[4 * part : 4 * part + 4] for r in kv[i : i + 2]])
    steps = len(pairs)
    wide = load_lines(pairs[0])
    ahead = [dot_nt(queries, k) for k, _ in wide]
    for step in range(steps):
        now, now_wide = ahead, wide
        if step + 1 < steps:
            wide = load_lines(pairs[step + 1])
            ahead = [dot_nt(queries, k) for k, _ in wide]
        state = absorb(state, now, now_wide)

    top, total, acc = state
    count = 4 * BEAMS
    pad = jnp.zeros((count - 3 * BEAMS, HEAD), F32)
    own_k = jnp.concatenate([halves[0][8 * BEAMS :], pad], 0).astype(BF16)
    own_v = jnp.concatenate([halves[1][8 * BEAMS :], pad], 0).astype(BF16)
    row = lax.broadcasted_iota(jnp.int32, (TOKENS, count), 0)
    key = lax.broadcasted_iota(jnp.int32, (TOKENS, count), 1)
    step = (row // (4 * BEAMS)) % 2
    beam = row % BEAMS
    slot = key // BEAMS
    first = jnp.logical_and(step == 0, slot == 0)
    second = jnp.logical_and(step == 1, jnp.logical_or(slot == 1, slot == 2))
    seen = jnp.logical_and(beam == key % BEAMS, jnp.logical_or(first, second))
    seen = jnp.logical_and(seen, beam // 4 == me)
    own = jnp.where(seen, dot_nt(queries, own_k), HIDE)
    peak = jnp.maximum(top, jnp.max(own, axis=-1, keepdims=True))
    alpha = jnp.exp2((top - peak) * EXP2_SCALE)
    w = jnp.exp2((own - peak[:, :1]) * EXP2_SCALE)
    total = total * alpha + jnp.sum(w, axis=-1, keepdims=True)
    acc = acc * alpha + dot_nn(w.astype(BF16), own_v)
    put_state(out, 0, 1, (peak, total, acc))


def merge_kernel(core, keep, got, beams_keep, beams_got, *refs):
    out, message = refs[:4], refs[4]
    me, first = core[0], core[2]
    for zh in range(4):
        message[zh, NEW:, WIDTH:] = jnp.zeros((NEW, HEAD), F32)
    for slot in range(GROUP + 1):
        if slot < GROUP:
            parts = [get_state(ref, slot, GROUP) for ref in (keep, got)]
        else:
            parts = [get_state(ref, 0, 1) for ref in (beams_keep, beams_got)]
        peak = jnp.maximum(parts[0][0], parts[1][0])
        a, b = [jnp.exp2((p[0] - peak) * EXP2_SCALE) for p in parts]
        total = parts[0][1] * a + parts[1][1] * b
        mixed = (parts[0][2] * a + parts[1][2] * b) / total
        if slot < GROUP:
            lanes = slice(slot * HEAD, (slot + 1) * HEAD)
            for zh in range(4):
                message[zh, :, lanes] = mixed[zh * 2 * NEW : (zh + 1) * 2 * NEW]
        else:
            for block in range(16):
                half, step, head = block // 8, (block // 4) % 2, block % 4
                at = step * GROUP + half * 4 + head
                tile = mixed[block * BEAMS : (block + 1) * BEAMS]
                tile = jnp.where(me == 0, tile[:4], tile[4:])
                for zh in range(4):
                    message[zh, at : at + 1, WIDTH:] = tile[zh : zh + 1]
    for k in range(4):
        out[k][...] = message[(first + k) % 4].astype(BF16)


def place_kernel(core, *refs):
    got, (stretch, decode) = refs[:4], refs[4:]
    zh = core[3]
    few = [jnp.zeros((NEW, HEAD), F32)] * 4
    for k in range(4):
        origin = (zh - k + 4) % 4
        lane = pl.multiple_of((origin // 2) * WIDTH, WIDTH)
        for low in range(2):
            row = pl.multiple_of(low * 2 * NEW + (origin % 2) * NEW, NEW)
            stretch[pl.ds(row, NEW), pl.ds(lane, WIDTH)] = got[k][
                low * NEW : (low + 1) * NEW, :WIDTH
            ]
        tail = got[k][:NEW, WIDTH:].astype(F32)
        few = [jnp.where(origin == i, tail, f) for i, f in enumerate(few)]
    for i in range(4):
        head, parity = i // 2, i % 2
        steps = [
            jnp.concatenate([few[i][s * GROUP + g : s * GROUP + g + 1] for g in range(GROUP)], 1)
            for s in range(2)
        ]
        decode[parity, :, head * WIDTH : (head + 1) * WIDTH] = jnp.concatenate(steps, 0).astype(BF16)


def shards(
    block_query_rows,
    block_key_rows,
    block_value_rows,
    stretch_pos,
    prompt_key_cache,
    prompt_value_cache,
    embed_table,
    query_weight,
    key_weight,
    value_weight,
    beam_tokens,
    parent_beam,
):
    zh, xi, yi, ci = (lax.axis_index(a) for a in ("zh", "x", "y", "c"))
    core = jnp.stack([ci, xi * 4 + yi, 2 * (zh // 2) + ci, zh]).astype(jnp.int32)

    packed = call(
        pack_kernel,
        jax.ShapeDtypeStruct((8, BOTH + 4 * NEW, 2 * HEAD), BF16),
        (),
        (prompt_key_cache, prompt_value_cache, block_key_rows, block_value_rows, block_query_rows),
        "pack",
    )
    packed = lax.all_to_all(packed, DEPTH, split_axis=0, concat_axis=0, tiled=True)

    depth = query_weight.shape[0]
    q_cols = query_weight.shape[1] // 4
    parts = jnp.concatenate(
        [
            query_weight.reshape(depth, 2, 2, q_cols),
            jnp.stack([key_weight.reshape(depth, 2, HEAD), value_weight.reshape(depth, 2, HEAD)], 2),
        ],
        -1,
    )
    parts = jnp.transpose(parts, (1, 2, 0, 3)).reshape(4, depth, q_cols + HEAD)
    weights = lax.all_to_all(parts, "x", split_axis=0, concat_axis=0, tiled=True)
    packed, weights = lax.optimization_barrier((packed, weights))

    def swap(v, axis, turn):
        pairs = []
        for at in range(8):
            i, c = at // 2, at % 2
            pairs.append((at, (i ^ (1 if c == turn else 3)) * 2 + c))
        return lax.ppermute(v, (axis, "c"), pairs)

    halves = [packed[:4, :BOTH][None], packed[4:, :BOTH][None]]
    near = []
    for half, axis in zip(halves, ("x", "y")):
        half = jnp.concatenate([half, swap(half, axis, 0)], 0)
        near.append(jnp.concatenate([half, swap(half, axis, 1)], 0))
    far = [swap(line, axis, 0) for line, axis in zip(near, ("y", "x"))]
    both = [jnp.concatenate(pair, 0) for pair in zip(near, far)]
    rest = [swap(line, axis, 1) for line, axis in zip(both, ("y", "x"))]
    q_other = lax.ppermute(packed[:, BOTH:], "c", [(0, 1), (1, 0)])

    pos = jnp.transpose(stretch_pos.reshape(4, 4, 4, 2, 2, NEW), (4, 1, 2, 0, 3, 5))
    halves = lax.dynamic_index_in_dim(pos.reshape(2, 4, 4, 2, TOKENS // 2), ci, 0, keepdims=False)
    pos = pos.reshape(32, TOKENS)

    def met(table, axis, index):
        table = jnp.moveaxis(table, axis, 0)
        table = jnp.where(index % 2 == 1, jnp.concatenate([table[1:2], table[:1], table[3:], table[2:3]], 0), table)
        table = jnp.where(index // 2 == 1, jnp.concatenate([table[2:], table[:2]], 0), table)
        one, three = jnp.where(ci == 0, table[1], table[3]), jnp.where(ci == 0, table[3], table[1])
        return jnp.moveaxis(jnp.stack([table[0], one, three, table[2]]), 0, axis)

    halves = met(met(halves, 0, xi), 1, yi)
    line_pos = jnp.concatenate(
        [
            jnp.transpose(halves[:, :, 0], (1, 0, 2)).reshape(4, 2 * TOKENS),
            halves[:, :, 1].reshape(4, 2 * TOKENS),
        ],
        0,
    )

    vocab_rows = embed_table.shape[0]
    beams = beam_tokens.shape[0]
    ids = jnp.transpose(beam_tokens.reshape(4, 4, 4, 2, 2), (4, 1, 2, 3, 0)).reshape(-1)
    looked = embed_table.at[ids % vocab_rows].get(mode="promise_in_bounds")
    looked = lax.all_to_all(
        jnp.broadcast_to(looked, (4,) + looked.shape), GRP, split_axis=0, concat_axis=0, tiled=True
    )
    hidden = call(
        hidden_kernel,
        jax.ShapeDtypeStruct((4, 2 * beams, HEAD), BF16),
        (),
        ((ids // vocab_rows)[:, None], looked),
        "hidden",
    )
    hidden = lax.all_to_all(hidden, "x", split_axis=0, concat_axis=0, tiled=True)

    beam_id = np.arange(beams, dtype=np.int32).reshape(4, 4, 4, 2).transpose(1, 2, 3, 0)
    parent = jnp.transpose(parent_beam.reshape(4, 4, 4, 2), (1, 2, 3, 0))
    part = call(
        project_kernel,
        jax.ShapeDtypeStruct((16, TILES, HEAD), F32),
        (),
        (parent.reshape(-1, 1), beam_id.reshape(1, -1), hidden, weights),
        "project",
        scratch=[
            pltpu.VMEM((2 * beams, q_cols + HEAD), F32),
            pltpu.VMEM((beams, HEAD), F32),
        ],
    )
    part = lax.all_to_all(part, ("zh", "y"), split_axis=0, concat_axis=0, tiled=True)
    part = call(sum_kernel, jax.ShapeDtypeStruct((TILES, HEAD), F32), (), (part,), "sum")
    sides = []
    for i in range(2):
        pairs = []
        for at in range(64):
            h, j, p, l, c = at >> 4, (at >> 3) & 1, (at >> 2) & 1, (at >> 1) & 1, at & 1
            pairs.append((at, (((2 * j + c) * 4 + h) * 2 + l) * 2 + (p ^ i)))
        sides.append(lax.ppermute(part, ("zh", "x", "zl", "c"), pairs))
    mine, theirs = sides

    def attend(starts, carry, pieces, name):
        work = 2 * GROUP * TOKENS * len(starts) * 32 * BOTH
        state = jax.ShapeDtypeStruct((GROUP * (TOKENS + 2), HEAD), F32)
        return call(
            lambda *refs: attend_kernel(starts, bool(carry), *refs),
            (state, state),
            (core,),
            (pos, line_pos, packed, q_other, *carry, *pieces),
            name,
            cost=pl.CostEstimate(
                flops=8 * work * HEAD, bytes_accessed=work // 4, transcendentals=work
            ),
        )

    carry = attend(((0, 0, 0),), (), near, "attend_near")
    carry = attend(((0, 0, 1),), carry, far, "attend_far")
    keep, send = attend(((0, 0, 2), (0, 1, 3)), carry, rest, "attend_rest")
    got = lax.ppermute(send, "c", [(0, 1), (1, 0)])
    beams_keep = call(
        decode_kernel,
        jax.ShapeDtypeStruct((TOKENS + 8, HEAD), F32),
        (core,),
        (mine, theirs, *near, *far, *rest),
        "decode",
        cost=pl.CostEstimate(
            flops=8 * TOKENS * 128 * BOTH * HEAD,
            bytes_accessed=512 * 128 * BOTH,
            transcendentals=TOKENS * 128 * BOTH,
        ),
    )
    beams_got = lax.ppermute(beams_keep, "c", [(0, 1), (1, 0)])
    messages = call(
        merge_kernel,
        [jax.ShapeDtypeStruct((2 * NEW, MESSAGE), BF16)] * 4,
        (core,),
        (keep, got, beams_keep, beams_got),
        "merge",
        scratch=[pltpu.VMEM((4, 2 * NEW, MESSAGE), F32)],
    )

    got = []
    for k in range(4):
        pairs = []
        for at in range(16):
            h1, h0, l, c = (at >> 3) & 1, (at >> 2) & 1, (at >> 1) & 1, at & 1
            pairs.append((at, (((2 * h1 + c + k) % 4) * 2 + l) * 2 + h0))
        got.append(lax.ppermute(messages[k], ("zh", "zl", "c"), pairs))
    return call(
        place_kernel,
        (
            jax.ShapeDtypeStruct((4 * NEW, 2 * WIDTH), BF16),
            jax.ShapeDtypeStruct((2, 2, 2 * WIDTH), BF16),
        ),
        (core,),
        got,
        "place",
    )


def solution(mesh):
    fine = Mesh(mesh.devices.reshape(4, 4, 4, 2, 2), ALL)
    return jax.shard_map(
        shards,
        mesh=fine,
        in_specs=(
            P(ALL, None),
            P(ALL, None),
            P(ALL, None),
            P(),
            P(ALL, None),
            P(ALL, None),
            P(GRP, SEQ),
            P(SEQ, GRP),
            P(SEQ, GRP),
            P(SEQ, GRP),
            P(),
            P(),
        ),
        out_specs=(P(SEQ, GRP), P(SEQ, None, GRP)),
        check_vma=False,
    )
```

```python
import jax
import jax.numpy as jnp
import numpy as np
from jax import lax
from jax.experimental import pallas as pl
from jax.experimental.pallas import tpu as pltpu
from jax.sharding import Mesh, PartitionSpec as P

HEAD = 128
GROUP = 8
WIDTH = GROUP * HEAD
EXP2_SCALE = HEAD ** (-0.5) * 1.4426950408889634
HIDE = -1e30
ALL = ("zh", "x", "y", "zl", "c")
SEQ = ("zh", "x", "y")
GRP = ("zl", "c")
DEPTH = ("zh", "zl")
OLD, NEW = 32, 16
BOTH = OLD + NEW
TOKENS = 8 * NEW
BEAMS = 8
TILES = 11 * BEAMS
STATS = 32
MESSAGE = WIDTH + HEAD
VMEM = pltpu.CompilerParams(vmem_limit_bytes=56 * 1024 * 1024)
SMEM_SPEC = pl.BlockSpec(memory_space=pltpu.SMEM)
VMEM_SPEC = pl.BlockSpec(memory_space=pltpu.VMEM)
BF16, F32 = jnp.bfloat16, jnp.float32


def dot_nt(a, b):
    return lax.dot_general(a, b, (((1,), (1,)), ((), ())), preferred_element_type=F32)


def dot_nn(a, b):
    return lax.dot_general(a, b, (((1,), (0,)), ((), ())), preferred_element_type=F32)


def call(kernel, out_shape, scalars, args, name, cost=None, scratch=()):
    return pl.pallas_call(
        kernel,
        out_shape=out_shape,
        in_specs=[SMEM_SPEC] * len(scalars) + [VMEM_SPEC] * len(args),
        out_specs=jax.tree.map(lambda _: VMEM_SPEC, out_shape),
        scratch_shapes=list(scratch),
        cost_estimate=cost,
        compiler_params=VMEM,
        name=name,
    )(*scalars, *args)


def head_of(plane):
    return 4 * (plane & 1) + 2 * ((plane >> 1) & 1) + (plane >> 2)


def pack_kernel(core, old_k, old_v, new_k, new_v, q, wq, wk, wv, kv_out, q_out, *w_out):
    for plane in range(8):
        head = head_of(plane)
        cols = slice(head * HEAD, (head + 1) * HEAD)
        kv_out[plane, :OLD, :HEAD] = old_k[:, cols]
        kv_out[plane, :OLD, HEAD:] = old_v[:, cols]
        kv_out[plane, OLD:, :HEAD] = new_k[:, cols]
        kv_out[plane, OLD:, HEAD:] = new_v[:, cols]
        for pair in range(4):
            at = head * WIDTH + pair * 2 * HEAD
            q_out[plane, pair * NEW : (pair + 1) * NEW, :] = q[:, at : at + 2 * HEAD]
    for k in range(4):
        part = core[4] ^ k
        w_out[k][:, : 4 * HEAD] = wq[:, pl.ds(pl.multiple_of(part * 4 * HEAD, 4 * HEAD), 4 * HEAD)]
        cols = pl.ds(pl.multiple_of((part // 2) * HEAD, HEAD), HEAD)
        w_out[k][:, 4 * HEAD :] = jnp.where(part % 2 == 0, wk[:, cols], wv[:, cols])


def hidden_kernel(core, owner, *refs):
    looked, out = refs[:4], refs[4]
    rows = jnp.zeros(out.shape, F32)
    for k in range(4):
        rows = rows + jnp.where(owner[...] == (core[5] ^ k), looked[k][...].astype(F32), 0.0)
    out[...] = rows.astype(BF16)


def project_kernel(parent, beam_id, *refs):
    hidden, weights, (out, total, extra) = refs[:4], refs[4:8], refs[8:]
    beams = extra.shape[0]
    pick = jnp.where(parent[...] == beam_id[...], 1.0, 0.0).astype(BF16)
    acc = acc_extra = 0.0
    for k in range(4):
        rows = hidden[k][...]
        acc = acc + dot_nn(rows, weights[k][...])
        chosen = dot_nn(pick, rows[:beams]).astype(BF16)
        acc_extra = acc_extra + dot_nn(chosen, weights[k][:, 4 * HEAD :])
    total[...] = acc
    extra[...] = acc_extra
    for chip in range(16):
        for step in range(2):
            rows = slice(step * beams + chip * BEAMS, step * beams + (chip + 1) * BEAMS)
            for head in range(4):
                at = (step * 4 + head) * BEAMS
                out[chip, at : at + BEAMS, :] = total[rows, head * HEAD : (head + 1) * HEAD]
            at = (8 + step) * BEAMS
            out[chip, at : at + BEAMS, :] = total[rows, 4 * HEAD :]
        out[chip, 10 * BEAMS :, :] = extra[chip * BEAMS : (chip + 1) * BEAMS, :]


def sum_kernel(parts, out):
    terms = [parts[i] for i in range(parts.shape[0])]
    while len(terms) > 1:
        terms = [a + b for a, b in zip(terms[::2], terms[1::2])]
    out[...] = terms[0]


def spread(ref, row):
    return jnp.transpose(jnp.broadcast_to(ref[row : row + 1, :], (TOKENS, HEAD)))


def load_lines(pair):
    wide = []
    for low, high in ((0, OLD), (OLD, BOTH)):
        count = 16 * (high - low)
        k = jnp.concatenate([r[:, :, low:high, :HEAD].reshape(count, HEAD) for r in pair], 0)
        v = jnp.concatenate([r[:, :, low:high, HEAD:].reshape(count, HEAD) for r in pair], 0)
        wide.append((k, jnp.concatenate([v, jnp.ones_like(v)], 1)))
    return wide


def absorb(state, tiles, wide):
    peak = jnp.maximum(
        jnp.max(tiles[0], axis=-1, keepdims=True), jnp.max(tiles[1], axis=-1, keepdims=True)
    )
    if state is None:
        peak = jnp.broadcast_to(peak, (TOKENS, HEAD))
    else:
        top, total, acc = state
        peak = jnp.maximum(top, peak)
        alpha = jnp.exp2((top - peak) * EXP2_SCALE)
    mixed = 0.0
    for s, (_, v) in zip(tiles, wide):
        w = jnp.exp2((s - peak[:, :1]) * EXP2_SCALE).astype(BF16)
        mixed = mixed + dot_nn(w, v)
    if state is None:
        return peak, mixed[:, HEAD:], mixed[:, :HEAD]
    return peak, mixed[:, HEAD:] + total * alpha, mixed[:, :HEAD] + acc * alpha


def put_state(ref, slot, state):
    top, total, acc = state
    ref[slot * TOKENS : (slot + 1) * TOKENS, :] = acc
    at = ref.shape[0] - STATS + slot
    ref[at : at + 1, :] = jnp.transpose(top)[:1]
    at = at + STATS // 2
    ref[at : at + 1, :] = jnp.transpose(total)[:1]


def get_state(ref, slot):
    at = ref.shape[0] - STATS + slot
    rows = slice(slot * TOKENS, (slot + 1) * TOKENS)
    return spread(ref, at), spread(ref, at + STATS // 2), ref[rows, :]


def attend_kernel(starts, resumed, earlier, core, pos, lines, own, other, *refs):
    if earlier:
        mine, theirs, refs = refs[0], refs[1], refs[2:]
    if resumed:
        states, refs = refs[:2], refs[2:]
    kv, (keep, send) = refs[:-2], refs[-2:]
    me, place = core[0], core[1]

    def column(which):
        row = pos[pl.ds(which * 16 + place, 1), :].astype(F32)
        return jnp.transpose(jnp.broadcast_to(row, (TOKENS, HEAD)))[:, :1]

    qpos = (column(me), column(1 - me))
    loaded = {}
    if earlier:
        halves, beams = beam_queries(me, mine, theirs)

    def scores(step, block):
        if step not in loaded and step < 0:
            first, part, _ = earlier[step]
            pair = [r.at[4 * part : 4 * part + 4] for r in kv[first : first + 2]]
            loaded[step] = (load_lines(pair), None)
        if step not in loaded:
            first, part, line = starts[step]
            kpos = jnp.concatenate([lines[line : line + 1], lines[4 + line : 5 + line]], 1)
            kpos = kpos.astype(F32)
            bias = [jnp.where(kpos <= p, 0.0, HIDE) for p in qpos]
            pair = [r.at[4 * part : 4 * part + 4] for r in kv[first : first + 2]]
            loaded[step] = (load_lines(pair), bias)
        wide, bias = loaded[step]
        if block == 2 * GROUP:
            return [dot_nt(beams, k) for k, _ in wide]
        head = block % GROUP
        lanes = slice((head % 2) * HEAD, (head % 2 + 1) * HEAD)
        at = (head // 2) * NEW
        q = (own, other)[block // GROUP][:, at : at + NEW, lanes].reshape(TOKENS, HEAD)
        return dot_nt(q, wide[0][0]), dot_nt(q, wide[1][0]) + bias[block // GROUP]

    state = {}
    blocks = 2 * GROUP + (1 if earlier else 0)
    order = [(step - len(earlier), 2 * GROUP) for step in range(len(earlier))]
    order += [(step, block) for step in range(len(starts)) for block in range(blocks)]
    ahead = scores(*order[0])
    for i, (step, block) in enumerate(order):
        now = ahead
        if i + 1 < len(order):
            ahead = scores(*order[i + 1])
        if step == 0 and resumed and block < 2 * GROUP:
            state[block] = get_state(states[block // GROUP], block % GROUP)
        state[block] = absorb(state.get(block), now, loaded[step][0])
        if step == len(starts) - 1:
            if block < 2 * GROUP:
                put_state((keep, send)[block // GROUP], block % GROUP, state[block])
            else:
                for ref in (keep, send):
                    put_state(ref, GROUP, absorb_own(me, halves, beams, state[block]))


def beam_queries(me, mine, theirs):
    halves = [jnp.where(me == 0, mine[...], theirs[...]), jnp.where(me == 0, theirs[...], mine[...])]
    return halves, jnp.concatenate([h[: 8 * BEAMS] for h in halves], 0).astype(BF16)


def absorb_own(me, halves, queries, state):
    top, total, acc = state
    count = 4 * BEAMS
    pad = jnp.zeros((count - 3 * BEAMS, HEAD), F32)
    own_k = jnp.concatenate([halves[0][8 * BEAMS :], pad], 0).astype(BF16)
    own_v = jnp.concatenate([halves[1][8 * BEAMS :], pad], 0).astype(BF16)
    row = lax.broadcasted_iota(jnp.int32, (TOKENS, count), 0)
    key = lax.broadcasted_iota(jnp.int32, (TOKENS, count), 1)
    step = (row // (4 * BEAMS)) % 2
    beam = row % BEAMS
    slot = key // BEAMS
    first = jnp.logical_and(step == 0, slot == 0)
    second = jnp.logical_and(step == 1, jnp.logical_or(slot == 1, slot == 2))
    seen = jnp.logical_and(beam == key % BEAMS, jnp.logical_or(first, second))
    seen = jnp.logical_and(seen, beam // 4 == me)
    own = jnp.where(seen, dot_nt(queries, own_k), HIDE)
    peak = jnp.maximum(top, jnp.max(own, axis=-1, keepdims=True))
    alpha = jnp.exp2((top - peak) * EXP2_SCALE)
    w = jnp.exp2((own - peak[:, :1]) * EXP2_SCALE)
    total = total * alpha + jnp.sum(w, axis=-1, keepdims=True)
    acc = acc * alpha + dot_nn(w.astype(BF16), own_v)
    return peak, total, acc


def merge_kernel(core, keep, got, *refs):
    out, message = refs[:4], refs[4]
    me, first = core[0], core[2]
    for zh in range(4):
        message[zh, NEW:, WIDTH:] = jnp.zeros((NEW, HEAD), F32)
    for slot in range(GROUP + 1):
        parts = [get_state(ref, slot) for ref in (keep, got)]
        peak = jnp.maximum(parts[0][0], parts[1][0])
        a, b = [jnp.exp2((p[0] - peak) * EXP2_SCALE) for p in parts]
        total = parts[0][1] * a + parts[1][1] * b
        mixed = (parts[0][2] * a + parts[1][2] * b) / total
        if slot < GROUP:
            lanes = slice(slot * HEAD, (slot + 1) * HEAD)
            for zh in range(4):
                message[zh, :, lanes] = mixed[zh * 2 * NEW : (zh + 1) * 2 * NEW]
        else:
            for block in range(16):
                half, step, head = block // 8, (block // 4) % 2, block % 4
                at = step * GROUP + half * 4 + head
                tile = mixed[block * BEAMS : (block + 1) * BEAMS]
                tile = jnp.where(me == 0, tile[:4], tile[4:])
                for zh in range(4):
                    message[zh, at : at + 1, WIDTH:] = tile[zh : zh + 1]
    for k in range(4):
        out[k][...] = message[(first + k) % 4].astype(BF16)


def place_kernel(core, *refs):
    got, (stretch, decode) = refs[:4], refs[4:]
    zh = core[3]
    few = [jnp.zeros((NEW, HEAD), F32)] * 4
    for k in range(4):
        origin = (zh - k + 4) % 4
        lane = pl.multiple_of((origin // 2) * WIDTH, WIDTH)
        for low in range(2):
            row = pl.multiple_of(low * 2 * NEW + (origin % 2) * NEW, NEW)
            stretch[pl.ds(row, NEW), pl.ds(lane, WIDTH)] = got[k][
                low * NEW : (low + 1) * NEW, :WIDTH
            ]
        tail = got[k][:NEW, WIDTH:].astype(F32)
        few = [jnp.where(origin == i, tail, f) for i, f in enumerate(few)]
    for i in range(4):
        head, parity = i // 2, i % 2
        steps = [
            jnp.concatenate([few[i][s * GROUP + g : s * GROUP + g + 1] for g in range(GROUP)], 1)
            for s in range(2)
        ]
        decode[parity, :, head * WIDTH : (head + 1) * WIDTH] = jnp.concatenate(steps, 0).astype(BF16)


def shards(
    block_query_rows,
    block_key_rows,
    block_value_rows,
    stretch_pos,
    prompt_key_cache,
    prompt_value_cache,
    embed_table,
    query_weight,
    key_weight,
    value_weight,
    beam_tokens,
    parent_beam,
):
    zh, xi, yi, ci = (lax.axis_index(a) for a in ("zh", "x", "y", "c"))
    core = jnp.stack([ci, xi * 4 + yi, 2 * (zh // 2) + ci, zh, xi, lax.axis_index(GRP)])
    core = core.astype(jnp.int32)

    depth = query_weight.shape[0]
    q_cols = query_weight.shape[1] // 4
    kv, q, *weights = call(
        pack_kernel,
        (
            jax.ShapeDtypeStruct((8, BOTH, 2 * HEAD), BF16),
            jax.ShapeDtypeStruct((8, 4 * NEW, 2 * HEAD), BF16),
            *[jax.ShapeDtypeStruct((depth, q_cols + HEAD), BF16)] * 4,
        ),
        (core,),
        (
            prompt_key_cache,
            prompt_value_cache,
            block_key_rows,
            block_value_rows,
            block_query_rows,
            query_weight,
            key_weight,
            value_weight,
        ),
        "pack",
    )
    kv = lax.all_to_all(kv, DEPTH, split_axis=0, concat_axis=0, tiled=True)

    def cross(v, axis, k):
        return lax.ppermute(v, axis, [(i, i ^ k) for i in range(4)])

    weights = [weights[0]] + [cross(weights[k], "x", k) for k in (1, 2, 3)]

    vocab_rows = embed_table.shape[0]
    beams = beam_tokens.shape[0]
    ids = jnp.transpose(beam_tokens.reshape(4, 4, 4, 2, 2), (4, 1, 2, 3, 0)).reshape(-1)
    looked = embed_table.at[ids % vocab_rows].get(mode="promise_in_bounds")
    looked = [looked] + [cross(looked, GRP, k) for k in (1, 2, 3)]
    kv, q = lax.optimization_barrier((kv, q))
    weights, looked = lax.optimization_barrier((weights, looked))

    def swap(v, axis, turn):
        pairs = []
        for at in range(8):
            i, c = at // 2, at % 2
            pairs.append((at, (i ^ (1 if c == turn else 3)) * 2 + c))
        return lax.ppermute(v, (axis, "c"), pairs)

    halves = [kv[:4][None], kv[4:][None]]
    near = []
    for half, axis in zip(halves, ("x", "y")):
        half = jnp.concatenate([half, swap(half, axis, 0)], 0)
        near.append(jnp.concatenate([half, swap(half, axis, 1)], 0))
    far = [swap(line, axis, 0) for line, axis in zip(near, ("y", "x"))]
    both = [jnp.concatenate(pair, 0) for pair in zip(near, far)]
    rest = [swap(line, axis, 1) for line, axis in zip(both, ("y", "x"))]
    q = lax.all_to_all(q, DEPTH, split_axis=0, concat_axis=0, tiled=True)
    q_other = lax.ppermute(q, "c", [(0, 1), (1, 0)])

    pos = jnp.transpose(stretch_pos.reshape(4, 4, 4, 2, 2, NEW), (4, 1, 2, 0, 3, 5))
    halves = lax.dynamic_index_in_dim(pos.reshape(2, 4, 4, 2, TOKENS // 2), ci, 0, keepdims=False)
    pos = pos.reshape(32, TOKENS)

    def met(table, axis, index):
        table = jnp.moveaxis(table, axis, 0)
        table = jnp.where(index % 2 == 1, jnp.concatenate([table[1:2], table[:1], table[3:], table[2:3]], 0), table)
        table = jnp.where(index // 2 == 1, jnp.concatenate([table[2:], table[:2]], 0), table)
        one, three = jnp.where(ci == 0, table[1], table[3]), jnp.where(ci == 0, table[3], table[1])
        return jnp.moveaxis(jnp.stack([table[0], one, three, table[2]]), 0, axis)

    halves = met(met(halves, 0, xi), 1, yi)
    line_pos = jnp.concatenate(
        [
            jnp.transpose(halves[:, :, 0], (1, 0, 2)).reshape(4, 2 * TOKENS),
            halves[:, :, 1].reshape(4, 2 * TOKENS),
        ],
        0,
    )

    hidden = call(
        hidden_kernel,
        jax.ShapeDtypeStruct((2 * beams, HEAD), BF16),
        (core,),
        ((ids // vocab_rows)[:, None], *looked),
        "hidden",
    )
    hidden = [hidden] + [cross(hidden, "x", k) for k in (1, 2, 3)]

    beam_id = np.arange(beams, dtype=np.int32).reshape(4, 4, 4, 2).transpose(1, 2, 3, 0)
    parent = jnp.transpose(parent_beam.reshape(4, 4, 4, 2), (1, 2, 3, 0))
    part = call(
        project_kernel,
        jax.ShapeDtypeStruct((16, TILES, HEAD), F32),
        (),
        (parent.reshape(-1, 1), beam_id.reshape(1, -1), *hidden, *weights),
        "project",
        scratch=[
            pltpu.VMEM((2 * beams, q_cols + HEAD), F32),
            pltpu.VMEM((beams, HEAD), F32),
        ],
    )
    part = lax.all_to_all(part, ("zh", "y"), split_axis=0, concat_axis=0, tiled=True)
    part = call(sum_kernel, jax.ShapeDtypeStruct((TILES, HEAD), F32), (), (part,), "sum")
    def attend(starts, carry, pieces, name, earlier=(), beam_rows=()):
        work = 2 * GROUP * TOKENS * len(starts) * 32 * BOTH
        slots = GROUP + (1 if earlier else 0)
        state = jax.ShapeDtypeStruct((slots * TOKENS + STATS, HEAD), F32)
        return call(
            lambda *refs: attend_kernel(starts, bool(carry), earlier, *refs),
            (state, state),
            (core,),
            (pos, line_pos, q, q_other, *beam_rows, *carry, *pieces),
            name,
            cost=pl.CostEstimate(
                flops=8 * work * HEAD, bytes_accessed=work // 4, transcendentals=work
            ),
        )

    carry = attend(((0, 0, 0),), (), near, "attend_near")
    carry = attend(((0, 0, 1),), carry, far, "attend_far")
    sides = []
    for i in range(2):
        pairs = []
        for at in range(64):
            h, j, p, l, c = at >> 4, (at >> 3) & 1, (at >> 2) & 1, (at >> 1) & 1, at & 1
            pairs.append((at, (((2 * j + c) * 4 + h) * 2 + l) * 2 + (p ^ i)))
        sides.append(lax.ppermute(part, ("zh", "x", "zl", "c"), pairs))
    keep, send = attend(
        ((4, 0, 2), (4, 1, 3)),
        carry,
        near + far + rest,
        "attend_rest",
        earlier=((0, 0, 0), (2, 0, 1)),
        beam_rows=sides,
    )
    got = lax.ppermute(send, "c", [(0, 1), (1, 0)])
    messages = call(
        merge_kernel,
        [jax.ShapeDtypeStruct((2 * NEW, MESSAGE), BF16)] * 4,
        (core,),
        (keep, got),
        "merge",
        scratch=[pltpu.VMEM((4, 2 * NEW, MESSAGE), F32)],
    )

    got = []
    for k in range(4):
        pairs = []
        for at in range(16):
            h1, h0, l, c = (at >> 3) & 1, (at >> 2) & 1, (at >> 1) & 1, at & 1
            pairs.append((at, (((2 * h1 + c + k) % 4) * 2 + l) * 2 + h0))
        got.append(lax.ppermute(messages[k], ("zh", "zl", "c"), pairs))
    return call(
        place_kernel,
        (
            jax.ShapeDtypeStruct((4 * NEW, 2 * WIDTH), BF16),
            jax.ShapeDtypeStruct((2, 2, 2 * WIDTH), BF16),
        ),
        (core,),
        got,
        "place",
    )


def solution(mesh):
    fine = Mesh(mesh.devices.reshape(4, 4, 4, 2, 2), ALL)
    return jax.shard_map(
        shards,
        mesh=fine,
        in_specs=(
            P(ALL, None),
            P(ALL, None),
            P(ALL, None),
            P(),
            P(ALL, None),
            P(ALL, None),
            P(GRP, SEQ),
            P(SEQ, GRP),
            P(SEQ, GRP),
            P(SEQ, GRP),
            P(),
            P(),
        ),
        out_specs=(P(SEQ, GRP), P(SEQ, None, GRP)),
        check_vma=False,
    )
```

```python
import jax
import jax.numpy as jnp
import numpy as np
from jax import lax
from jax.experimental import pallas as pl
from jax.experimental.pallas import tpu as pltpu
from jax.sharding import Mesh, PartitionSpec as P

HEAD = 128
GROUP = 8
WIDTH = GROUP * HEAD
EXP2_SCALE = HEAD ** (-0.5) * 1.4426950408889634
HIDE = -1e30
ALL = ("zh", "x", "y", "zl", "c")
SEQ = ("zh", "x", "y")
GRP = ("zl", "c")
DEPTH = ("zh", "zl")
OLD, NEW = 32, 16
BOTH = OLD + NEW
TOKENS = 8 * NEW
BEAMS = 8
TILES = 11 * BEAMS
STATS = 32
MESSAGE = WIDTH + HEAD
VMEM = pltpu.CompilerParams(vmem_limit_bytes=56 * 1024 * 1024)
SMEM_SPEC = pl.BlockSpec(memory_space=pltpu.SMEM)
VMEM_SPEC = pl.BlockSpec(memory_space=pltpu.VMEM)
BF16, F32 = jnp.bfloat16, jnp.float32


def dot_nt(a, b):
    return lax.dot_general(a, b, (((1,), (1,)), ((), ())), preferred_element_type=F32)


def dot_nn(a, b):
    return lax.dot_general(a, b, (((1,), (0,)), ((), ())), preferred_element_type=F32)


def call(kernel, out_shape, scalars, args, name, cost=None, scratch=()):
    return pl.pallas_call(
        kernel,
        out_shape=out_shape,
        in_specs=[SMEM_SPEC] * len(scalars) + [VMEM_SPEC] * len(args),
        out_specs=jax.tree.map(lambda _: VMEM_SPEC, out_shape),
        scratch_shapes=list(scratch),
        cost_estimate=cost,
        compiler_params=VMEM,
        name=name,
    )(*scalars, *args)


def head_of(plane):
    return 4 * (plane & 1) + 2 * ((plane >> 1) & 1) + (plane >> 2)


def pack_kernel(core, old_k, old_v, new_k, new_v, q, wq, wk, wv, out, *w_out):
    for plane in range(8):
        head = head_of(plane)
        cols = slice(head * HEAD, (head + 1) * HEAD)
        out[plane, :OLD, :HEAD] = old_k[:, cols]
        out[plane, :OLD, HEAD:] = old_v[:, cols]
        out[plane, OLD:BOTH, :HEAD] = new_k[:, cols]
        out[plane, OLD:BOTH, HEAD:] = new_v[:, cols]
        for pair in range(4):
            at = head * WIDTH + pair * 2 * HEAD
            out[plane, BOTH + pair * NEW : BOTH + (pair + 1) * NEW, :] = q[:, at : at + 2 * HEAD]
    for k in range(4):
        part = core[2] ^ k
        w_out[k][:, : 4 * HEAD] = wq[:, pl.ds(pl.multiple_of(part * 4 * HEAD, 4 * HEAD), 4 * HEAD)]
        cols = pl.ds(pl.multiple_of((part // 2) * HEAD, HEAD), HEAD)
        w_out[k][:, 4 * HEAD :] = jnp.where(part % 2 == 0, wk[:, cols], wv[:, cols])


def hidden_kernel(core, owner, *refs):
    looked, out = refs[:4], refs[4]
    rows = jnp.zeros(out.shape, F32)
    for k in range(4):
        rows = rows + jnp.where(owner[...] == (core[3] ^ k), looked[k][...].astype(F32), 0.0)
    out[...] = rows.astype(BF16)


def project_kernel(parent, beam_id, *refs):
    hidden, weights, (out, total, extra) = refs[:4], refs[4:8], refs[8:]
    beams = extra.shape[0]
    pick = jnp.where(parent[...] == beam_id[...], 1.0, 0.0).astype(BF16)
    acc = acc_extra = 0.0
    for k in range(4):
        rows = hidden[k][...]
        acc = acc + dot_nn(rows, weights[k][...])
        chosen = dot_nn(pick, rows[:beams]).astype(BF16)
        acc_extra = acc_extra + dot_nn(chosen, weights[k][:, 4 * HEAD :])
    total[...] = acc
    extra[...] = acc_extra
    for chip in range(16):
        for step in range(2):
            rows = slice(step * beams + chip * BEAMS, step * beams + (chip + 1) * BEAMS)
            for head in range(4):
                at = (step * 4 + head) * BEAMS
                out[chip, at : at + BEAMS, :] = total[rows, head * HEAD : (head + 1) * HEAD]
            at = (8 + step) * BEAMS
            out[chip, at : at + BEAMS, :] = total[rows, 4 * HEAD :]
        out[chip, 10 * BEAMS :, :] = extra[chip * BEAMS : (chip + 1) * BEAMS, :]


def sum_kernel(parts, out):
    terms = [parts[i] for i in range(parts.shape[0])]
    while len(terms) > 1:
        terms = [a + b for a, b in zip(terms[::2], terms[1::2])]
    out[...] = terms[0]


def spread(ref, row):
    return jnp.transpose(jnp.broadcast_to(ref[row : row + 1, :], (TOKENS, HEAD)))


def load_lines(pair):
    wide = []
    for low, high in ((0, OLD), (OLD, BOTH)):
        count = 16 * (high - low)
        k = jnp.concatenate([r[:, :, low:high, :HEAD].reshape(count, HEAD) for r in pair], 0)
        v = jnp.concatenate([r[:, :, low:high, HEAD:].reshape(count, HEAD) for r in pair], 0)
        wide.append((k, jnp.concatenate([v, jnp.ones_like(v)], 1)))
    return wide


def absorb(state, tiles, wide):
    peak = jnp.maximum(
        jnp.max(tiles[0], axis=-1, keepdims=True), jnp.max(tiles[1], axis=-1, keepdims=True)
    )
    if state is None:
        peak = jnp.broadcast_to(peak, (TOKENS, HEAD))
    else:
        top, total, acc = state
        peak = jnp.maximum(top, peak)
        alpha = jnp.exp2((top - peak) * EXP2_SCALE)
    mixed = 0.0
    for s, (_, v) in zip(tiles, wide):
        w = jnp.exp2((s - peak[:, :1]) * EXP2_SCALE).astype(BF16)
        mixed = mixed + dot_nn(w, v)
    if state is None:
        return peak, mixed[:, HEAD:], mixed[:, :HEAD]
    return peak, mixed[:, HEAD:] + total * alpha, mixed[:, :HEAD] + acc * alpha


def put_state(ref, slot, state):
    top, total, acc = state
    ref[slot * TOKENS : (slot + 1) * TOKENS, :] = acc
    at = ref.shape[0] - STATS + slot
    ref[at : at + 1, :] = jnp.transpose(top)[:1]
    at = at + STATS // 2
    ref[at : at + 1, :] = jnp.transpose(total)[:1]


def get_state(ref, slot):
    at = ref.shape[0] - STATS + slot
    rows = slice(slot * TOKENS, (slot + 1) * TOKENS)
    return spread(ref, at), spread(ref, at + STATS // 2), ref[rows, :]


def attend_kernel(starts, resumed, earlier, core, pos, lines, own, other, *refs):
    if earlier:
        mine, theirs, refs = refs[0], refs[1], refs[2:]
    if resumed:
        states, refs = refs[:2], refs[2:]
    kv, (keep, send) = refs[:-2], refs[-2:]
    me, place = core[0], core[1]

    def column(which):
        row = pos[pl.ds(which * 16 + place, 1), :].astype(F32)
        return jnp.transpose(jnp.broadcast_to(row, (TOKENS, HEAD)))[:, :1]

    qpos = (column(me), column(1 - me))
    loaded = {}
    if earlier:
        halves, beams = beam_queries(me, mine, theirs)

    def scores(step, block):
        if step not in loaded and step < 0:
            first, part, _ = earlier[step]
            pair = [r.at[4 * part : 4 * part + 4] for r in kv[first : first + 2]]
            loaded[step] = (load_lines(pair), None)
        if step not in loaded:
            first, part, line = starts[step]
            kpos = jnp.concatenate([lines[line : line + 1], lines[4 + line : 5 + line]], 1)
            kpos = kpos.astype(F32)
            bias = [jnp.where(kpos <= p, 0.0, HIDE) for p in qpos]
            pair = [r.at[4 * part : 4 * part + 4] for r in kv[first : first + 2]]
            loaded[step] = (load_lines(pair), bias)
        wide, bias = loaded[step]
        if block == 2 * GROUP:
            return [dot_nt(beams, k) for k, _ in wide]
        head = block % GROUP
        lanes = slice((head % 2) * HEAD, (head % 2 + 1) * HEAD)
        at = BOTH + (head // 2) * NEW
        q = (own, other)[block // GROUP][:, at : at + NEW, lanes].reshape(TOKENS, HEAD)
        return dot_nt(q, wide[0][0]), dot_nt(q, wide[1][0]) + bias[block // GROUP]

    state = {}
    blocks = 2 * GROUP + (1 if earlier else 0)
    order = [(step - len(earlier), 2 * GROUP) for step in range(len(earlier))]
    order += [(step, block) for step in range(len(starts)) for block in range(blocks)]
    ahead = scores(*order[0])
    for i, (step, block) in enumerate(order):
        now = ahead
        if i + 1 < len(order):
            ahead = scores(*order[i + 1])
        if step == 0 and resumed and block < 2 * GROUP:
            state[block] = get_state(states[block // GROUP], block % GROUP)
        state[block] = absorb(state.get(block), now, loaded[step][0])
        if step == len(starts) - 1:
            if block < 2 * GROUP:
                put_state((keep, send)[block // GROUP], block % GROUP, state[block])
            else:
                for ref in (keep, send):
                    put_state(ref, GROUP, absorb_own(me, halves, beams, state[block]))


def beam_queries(me, mine, theirs):
    halves = [jnp.where(me == 0, mine[...], theirs[...]), jnp.where(me == 0, theirs[...], mine[...])]
    return halves, jnp.concatenate([h[: 8 * BEAMS] for h in halves], 0).astype(BF16)


def absorb_own(me, halves, queries, state):
    top, total, acc = state
    count = 4 * BEAMS
    pad = jnp.zeros((count - 3 * BEAMS, HEAD), F32)
    own_k = jnp.concatenate([halves[0][8 * BEAMS :], pad], 0).astype(BF16)
    own_v = jnp.concatenate([halves[1][8 * BEAMS :], pad], 0).astype(BF16)
    row = lax.broadcasted_iota(jnp.int32, (TOKENS, count), 0)
    key = lax.broadcasted_iota(jnp.int32, (TOKENS, count), 1)
    step = (row // (4 * BEAMS)) % 2
    beam = row % BEAMS
    slot = key // BEAMS
    first = jnp.logical_and(step == 0, slot == 0)
    second = jnp.logical_and(step == 1, jnp.logical_or(slot == 1, slot == 2))
    seen = jnp.logical_and(beam == key % BEAMS, jnp.logical_or(first, second))
    seen = jnp.logical_and(seen, beam // 4 == me)
    own = jnp.where(seen, dot_nt(queries, own_k), HIDE)
    peak = jnp.maximum(top, jnp.max(own, axis=-1, keepdims=True))
    alpha = jnp.exp2((top - peak) * EXP2_SCALE)
    w = jnp.exp2((own - peak[:, :1]) * EXP2_SCALE)
    total = total * alpha + jnp.sum(w, axis=-1, keepdims=True)
    acc = acc * alpha + dot_nn(w.astype(BF16), own_v)
    return peak, total, acc


def merge_kernel(core, keep, got, out, message):
    me = core[0]
    for zh in range(4):
        message[zh, NEW:, WIDTH:] = jnp.zeros((NEW, HEAD), F32)
    for slot in range(GROUP + 1):
        parts = [get_state(ref, slot) for ref in (keep, got)]
        peak = jnp.maximum(parts[0][0], parts[1][0])
        a, b = [jnp.exp2((p[0] - peak) * EXP2_SCALE) for p in parts]
        total = parts[0][1] * a + parts[1][1] * b
        mixed = (parts[0][2] * a + parts[1][2] * b) / total
        if slot < GROUP:
            lanes = slice(slot * HEAD, (slot + 1) * HEAD)
            for zh in range(4):
                message[zh, :, lanes] = mixed[zh * 2 * NEW : (zh + 1) * 2 * NEW]
        else:
            for block in range(16):
                half, step, head = block // 8, (block // 4) % 2, block % 4
                at = step * GROUP + half * 4 + head
                tile = mixed[block * BEAMS : (block + 1) * BEAMS]
                tile = jnp.where(me == 0, tile[:4], tile[4:])
                for zh in range(4):
                    message[zh, at : at + 1, WIDTH:] = tile[zh : zh + 1]
    out[...] = message[...].astype(BF16)


def place_kernel(core, near, far, stretch, decode):
    me = core[0]
    for j in range(2):
        lanes = slice(j * WIDTH, (j + 1) * WIDTH)
        own, other = near[2 * j + me], far[2 * j + me]
        for side, parity in ((own, me), (other, 1 - me)):
            for low in range(2):
                row = pl.multiple_of(low * 2 * NEW + parity * NEW, NEW)
                stretch[pl.ds(row, NEW), lanes] = side[low * NEW : (low + 1) * NEW, :WIDTH]
        tails = [v[:NEW, WIDTH:].astype(F32) for v in (own, other)]
        for parity in range(2):
            few = jnp.where(me == parity, tails[0], tails[1])
            steps = [
                jnp.concatenate([few[s * GROUP + g : s * GROUP + g + 1] for g in range(GROUP)], 1)
                for s in range(2)
            ]
            decode[parity, :, lanes] = jnp.concatenate(steps, 0).astype(BF16)


def shards(
    block_query_rows,
    block_key_rows,
    block_value_rows,
    stretch_pos,
    prompt_key_cache,
    prompt_value_cache,
    embed_table,
    query_weight,
    key_weight,
    value_weight,
    beam_tokens,
    parent_beam,
):
    xi, yi, ci = (lax.axis_index(a) for a in ("x", "y", "c"))
    core = jnp.stack([ci, xi * 4 + yi, xi, lax.axis_index(GRP)])
    core = core.astype(jnp.int32)

    depth = query_weight.shape[0]
    q_cols = query_weight.shape[1] // 4
    packed, *weights = call(
        pack_kernel,
        (
            jax.ShapeDtypeStruct((8, BOTH + 4 * NEW, 2 * HEAD), BF16),
            *[jax.ShapeDtypeStruct((depth, q_cols + HEAD), BF16)] * 4,
        ),
        (core,),
        (
            prompt_key_cache,
            prompt_value_cache,
            block_key_rows,
            block_value_rows,
            block_query_rows,
            query_weight,
            key_weight,
            value_weight,
        ),
        "pack",
    )
    packed = lax.all_to_all(packed, DEPTH, split_axis=0, concat_axis=0, tiled=True)

    def cross(v, axis, k):
        return lax.ppermute(v, axis, [(i, i ^ k) for i in range(4)])

    weights = [weights[0]] + [cross(weights[k], "x", k) for k in (1, 2, 3)]

    vocab_rows = embed_table.shape[0]
    beams = beam_tokens.shape[0]
    ids = jnp.transpose(beam_tokens.reshape(4, 4, 4, 2, 2), (4, 1, 2, 3, 0)).reshape(-1)
    looked = embed_table.at[ids % vocab_rows].get(mode="promise_in_bounds")
    looked = [looked] + [cross(looked, GRP, k) for k in (1, 2, 3)]
    weights, looked = lax.optimization_barrier((weights, looked))

    def swap(v, axis, turn):
        pairs = []
        for at in range(8):
            i, c = at // 2, at % 2
            pairs.append((at, (i ^ (1 if c == turn else 3)) * 2 + c))
        return lax.ppermute(v, (axis, "c"), pairs)

    halves = [packed[:4, :BOTH][None], packed[4:, :BOTH][None]]
    got = [swap(half, axis, 0) for half, axis in zip(halves, ("x", "y"))]
    got, looked = lax.optimization_barrier((got, looked))
    halves = [jnp.concatenate(pair, 0) for pair in zip(halves, got)]
    near = [
        jnp.concatenate([half, swap(half, axis, 1)], 0) for half, axis in zip(halves, ("x", "y"))
    ]
    packed_other = lax.ppermute(packed, "c", [(0, 1), (1, 0)])

    pos = jnp.transpose(stretch_pos.reshape(4, 4, 4, 2, 2, NEW), (4, 1, 2, 0, 3, 5))
    halves = lax.dynamic_index_in_dim(pos.reshape(2, 4, 4, 2, TOKENS // 2), ci, 0, keepdims=False)
    pos = pos.reshape(32, TOKENS)

    def met(table, axis, index):
        table = jnp.moveaxis(table, axis, 0)
        table = jnp.where(index % 2 == 1, jnp.concatenate([table[1:2], table[:1], table[3:], table[2:3]], 0), table)
        table = jnp.where(index // 2 == 1, jnp.concatenate([table[2:], table[:2]], 0), table)
        one, three = jnp.where(ci == 0, table[1], table[3]), jnp.where(ci == 0, table[3], table[1])
        return jnp.moveaxis(jnp.stack([table[0], one, three, table[2]]), 0, axis)

    halves = met(met(halves, 0, xi), 1, yi)
    line_pos = jnp.concatenate(
        [
            jnp.transpose(halves[:, :, 0], (1, 0, 2)).reshape(4, 2 * TOKENS),
            halves[:, :, 1].reshape(4, 2 * TOKENS),
        ],
        0,
    )

    hidden = call(
        hidden_kernel,
        jax.ShapeDtypeStruct((2 * beams, HEAD), BF16),
        (core,),
        ((ids // vocab_rows)[:, None], *looked),
        "hidden",
    )
    hidden = [hidden] + [cross(hidden, "x", k) for k in (1, 2, 3)]

    near, hidden = lax.optimization_barrier((near, hidden))
    far = [swap(line, axis, 0) for line, axis in zip(near, ("y", "x"))]
    both = [jnp.concatenate(pair, 0) for pair in zip(near, far)]

    beam_id = np.arange(beams, dtype=np.int32).reshape(4, 4, 4, 2).transpose(1, 2, 3, 0)
    parent = jnp.transpose(parent_beam.reshape(4, 4, 4, 2), (1, 2, 3, 0))
    part = call(
        project_kernel,
        jax.ShapeDtypeStruct((16, TILES, HEAD), F32),
        (),
        (parent.reshape(-1, 1), beam_id.reshape(1, -1), *hidden, *weights),
        "project",
        scratch=[
            pltpu.VMEM((2 * beams, q_cols + HEAD), F32),
            pltpu.VMEM((beams, HEAD), F32),
        ],
    )
    part, both = lax.optimization_barrier((part, both))
    rest = [swap(line, axis, 1) for line, axis in zip(both, ("y", "x"))]
    part = lax.all_to_all(part, ("zh", "y"), split_axis=0, concat_axis=0, tiled=True)
    def attend(starts, carry, pieces, name, earlier=(), beam_rows=()):
        work = 2 * GROUP * TOKENS * len(starts) * 32 * BOTH
        slots = GROUP + (1 if earlier else 0)
        state = jax.ShapeDtypeStruct((slots * TOKENS + STATS, HEAD), F32)
        return call(
            lambda *refs: attend_kernel(starts, bool(carry), earlier, *refs),
            (state, state),
            (core,),
            (pos, line_pos, packed, packed_other, *beam_rows, *carry, *pieces),
            name,
            cost=pl.CostEstimate(
                flops=8 * work * HEAD, bytes_accessed=work // 4, transcendentals=work
            ),
        )

    carry = attend(((0, 0, 0), (2, 0, 1)), (), near + far, "attend_near")
    carry, part = lax.optimization_barrier((carry, part))
    part = call(sum_kernel, jax.ShapeDtypeStruct((TILES, HEAD), F32), (), (part,), "sum")
    sides = []
    for i in range(2):
        pairs = []
        for at in range(64):
            h, j, p, l, c = at >> 4, (at >> 3) & 1, (at >> 2) & 1, (at >> 1) & 1, at & 1
            pairs.append((at, (((2 * j + c) * 4 + h) * 2 + l) * 2 + (p ^ i)))
        sides.append(lax.ppermute(part, ("zh", "x", "zl", "c"), pairs))
    keep, send = attend(
        ((4, 0, 2), (4, 1, 3)),
        carry,
        near + far + rest,
        "attend_rest",
        earlier=((0, 0, 0), (2, 0, 1)),
        beam_rows=sides,
    )
    got = lax.ppermute(send, "c", [(0, 1), (1, 0)])
    messages = call(
        merge_kernel,
        jax.ShapeDtypeStruct((4, 2 * NEW, MESSAGE), BF16),
        (core,),
        (keep, got),
        "merge",
        scratch=[pltpu.VMEM((4, 2 * NEW, MESSAGE), F32)],
    )

    near = lax.all_to_all(messages, "zh", split_axis=0, concat_axis=0, tiled=True)
    far = lax.ppermute(near, "c", [(0, 1), (1, 0)])
    return call(
        place_kernel,
        (
            jax.ShapeDtypeStruct((4 * NEW, 2 * WIDTH), BF16),
            jax.ShapeDtypeStruct((2, 2, 2 * WIDTH), BF16),
        ),
        (core,),
        (near, far),
        "place",
    )


def solution(mesh):
    fine = Mesh(mesh.devices.reshape(4, 4, 4, 2, 2), ALL)
    return jax.shard_map(
        shards,
        mesh=fine,
        in_specs=(
            P(ALL, None),
            P(ALL, None),
            P(ALL, None),
            P(),
            P(ALL, None),
            P(ALL, None),
            P(GRP, SEQ),
            P(SEQ, GRP),
            P(SEQ, GRP),
            P(SEQ, GRP),
            P(),
            P(),
        ),
        out_specs=(P(SEQ, GRP), P(SEQ, None, GRP)),
        check_vma=False,
    )
```

```python
import jax
import jax.numpy as jnp
import numpy as np
from jax import lax
from jax.experimental import pallas as pl
from jax.experimental.pallas import tpu as pltpu
from jax.sharding import Mesh, PartitionSpec as P

HEAD = 128
GROUP = 8
WIDTH = GROUP * HEAD
EXP2_SCALE = HEAD ** (-0.5) * 1.4426950408889634
HIDE = -1e30
ALL = ("zh", "x", "y", "zl", "c")
SEQ = ("zh", "x", "y")
GRP = ("zl", "c")
DEPTH = ("zh", "zl")
OLD, NEW = 32, 16
BOTH = OLD + NEW
TOKENS = 8 * NEW
BEAMS = 8
TILES = 11 * BEAMS
STATS = 32
MESSAGE = WIDTH + HEAD
VMEM = pltpu.CompilerParams(vmem_limit_bytes=56 * 1024 * 1024)
SMEM_SPEC = pl.BlockSpec(memory_space=pltpu.SMEM)
VMEM_SPEC = pl.BlockSpec(memory_space=pltpu.VMEM)
BF16, F32 = jnp.bfloat16, jnp.float32


def dot_nt(a, b):
    return lax.dot_general(a, b, (((1,), (1,)), ((), ())), preferred_element_type=F32)


def dot_nn(a, b):
    return lax.dot_general(a, b, (((1,), (0,)), ((), ())), preferred_element_type=F32)


def call(kernel, out_shape, scalars, args, name, cost=None, scratch=()):
    return pl.pallas_call(
        kernel,
        out_shape=out_shape,
        in_specs=[SMEM_SPEC] * len(scalars) + [VMEM_SPEC] * len(args),
        out_specs=jax.tree.map(lambda _: VMEM_SPEC, out_shape),
        scratch_shapes=list(scratch),
        cost_estimate=cost,
        compiler_params=VMEM,
        name=name,
    )(*scalars, *args)


def head_of(plane):
    return 4 * (plane & 1) + 2 * ((plane >> 1) & 1) + (plane >> 2)


def pack_kernel(core, old_k, old_v, new_k, new_v, q, wq, wk, wv, out, *w_out):
    for plane in range(8):
        head = head_of(plane)
        cols = slice(head * HEAD, (head + 1) * HEAD)
        out[plane, :OLD, :HEAD] = old_k[:, cols]
        out[plane, :OLD, HEAD:] = old_v[:, cols]
        out[plane, OLD:BOTH, :HEAD] = new_k[:, cols]
        out[plane, OLD:BOTH, HEAD:] = new_v[:, cols]
        for pair in range(4):
            at = head * WIDTH + pair * 2 * HEAD
            out[plane, BOTH + pair * NEW : BOTH + (pair + 1) * NEW, :] = q[:, at : at + 2 * HEAD]
    for k in range(4):
        part = core[2] ^ k
        w_out[k][:, : 4 * HEAD] = wq[:, pl.ds(pl.multiple_of(part * 4 * HEAD, 4 * HEAD), 4 * HEAD)]
        cols = pl.ds(pl.multiple_of((part // 2) * HEAD, HEAD), HEAD)
        w_out[k][:, 4 * HEAD :] = jnp.where(part % 2 == 0, wk[:, cols], wv[:, cols])


def spread(ref, row):
    return jnp.transpose(jnp.broadcast_to(ref[row : row + 1, :].astype(F32), (TOKENS, HEAD)))


def hidden_kernel(core, owner, *refs):
    looked, out = refs[:4], refs[4]
    for part in range(owner.shape[0]):
        at = slice(part * HEAD, (part + 1) * HEAD)
        who = spread(owner, part)
        rows = jnp.zeros((HEAD, HEAD), F32)
        for k in range(4):
            from_k = (core[3] ^ k).astype(F32)
            rows = rows + jnp.where(who == from_k, looked[k][at, :].astype(F32), 0.0)
        out[at, :] = rows.astype(BF16)


def project_kernel(parent, beam_id, *refs):
    hidden, weights, (out, total, extra) = refs[:4], refs[4:8], refs[8:]
    beams = extra.shape[0]
    pick = jnp.where(spread(parent, 0) == beam_id[...].astype(F32), 1.0, 0.0).astype(BF16)
    acc = acc_extra = 0.0
    for k in range(4):
        rows = hidden[k][...]
        acc = acc + dot_nn(rows, weights[k][...])
        chosen = dot_nn(pick, rows[:beams]).astype(BF16)
        acc_extra = acc_extra + dot_nn(chosen, weights[k][:, 4 * HEAD :])
    total[...] = acc
    extra[...] = acc_extra
    for chip in range(16):
        for step in range(2):
            rows = slice(step * beams + chip * BEAMS, step * beams + (chip + 1) * BEAMS)
            for head in range(4):
                at = (step * 4 + head) * BEAMS
                out[chip, at : at + BEAMS, :] = total[rows, head * HEAD : (head + 1) * HEAD]
            at = (8 + step) * BEAMS
            out[chip, at : at + BEAMS, :] = total[rows, 4 * HEAD :]
        out[chip, 10 * BEAMS :, :] = extra[chip * BEAMS : (chip + 1) * BEAMS, :]


def sum_kernel(parts, out):
    terms = [parts[i] for i in range(parts.shape[0])]
    while len(terms) > 1:
        terms = [a + b for a, b in zip(terms[::2], terms[1::2])]
    out[...] = terms[0]


def load_lines(pair):
    wide = []
    for low, high in ((0, OLD), (OLD, BOTH)):
        count = 16 * (high - low)
        k = jnp.concatenate([r[:, :, low:high, :HEAD].reshape(count, HEAD) for r in pair], 0)
        v = jnp.concatenate([r[:, :, low:high, HEAD:].reshape(count, HEAD) for r in pair], 0)
        wide.append((k, jnp.concatenate([v, jnp.ones_like(v)], 1)))
    return wide


def absorb(state, tiles, wide):
    peak = jnp.maximum(
        jnp.max(tiles[0], axis=-1, keepdims=True), jnp.max(tiles[1], axis=-1, keepdims=True)
    )
    if state is None:
        peak = jnp.broadcast_to(peak, (TOKENS, HEAD))
    else:
        top, total, acc = state
        peak = jnp.maximum(top, peak)
        alpha = jnp.exp2((top - peak) * EXP2_SCALE)
    mixed = 0.0
    for s, (_, v) in zip(tiles, wide):
        w = jnp.exp2((s - peak[:, :1]) * EXP2_SCALE).astype(BF16)
        mixed = mixed + dot_nn(w, v)
    if state is None:
        return peak, mixed[:, HEAD:], mixed[:, :HEAD]
    return peak, mixed[:, HEAD:] + total * alpha, mixed[:, :HEAD] + acc * alpha


def put_state(ref, slot, state):
    top, total, acc = state
    ref[slot * TOKENS : (slot + 1) * TOKENS, :] = acc
    at = ref.shape[0] - STATS + slot
    ref[at : at + 1, :] = jnp.transpose(top)[:1]
    at = at + STATS // 2
    ref[at : at + 1, :] = jnp.transpose(total)[:1]


def get_state(ref, slot):
    at = ref.shape[0] - STATS + slot
    rows = slice(slot * TOKENS, (slot + 1) * TOKENS)
    return spread(ref, at), spread(ref, at + STATS // 2), ref[rows, :]


def attend_kernel(starts, resumed, earlier, core, pos, lines, own, other, *refs):
    if earlier:
        mine, theirs, refs = refs[0], refs[1], refs[2:]
    if resumed:
        states, refs = refs[:2], refs[2:]
    kv, (keep, send) = refs[:-2], refs[-2:]
    me, place = core[0], core[1]

    def column(which):
        row = pos[pl.ds(which * 16 + place, 1), :].astype(F32)
        return jnp.transpose(jnp.broadcast_to(row, (TOKENS, HEAD)))[:, :1]

    qpos = (column(me), column(1 - me))
    loaded = {}
    if earlier:
        halves, beams = beam_queries(me, mine, theirs)

    def scores(step, block):
        if step not in loaded and step < 0:
            first, part, _ = earlier[step]
            pair = [r.at[4 * part : 4 * part + 4] for r in kv[first : first + 2]]
            loaded[step] = (load_lines(pair), None)
        if step not in loaded:
            first, part, line = starts[step]
            kpos = jnp.concatenate([lines[line : line + 1], lines[4 + line : 5 + line]], 1)
            kpos = kpos.astype(F32)
            bias = [jnp.where(kpos <= p, 0.0, HIDE) for p in qpos]
            pair = [r.at[4 * part : 4 * part + 4] for r in kv[first : first + 2]]
            loaded[step] = (load_lines(pair), bias)
        wide, bias = loaded[step]
        if block == 2 * GROUP:
            return [dot_nt(beams, k) for k, _ in wide]
        head = block % GROUP
        lanes = slice((head % 2) * HEAD, (head % 2 + 1) * HEAD)
        at = BOTH + (head // 2) * NEW
        q = (own, other)[block // GROUP][:, at : at + NEW, lanes].reshape(TOKENS, HEAD)
        return dot_nt(q, wide[0][0]), dot_nt(q, wide[1][0]) + bias[block // GROUP]

    state = {}
    blocks = 2 * GROUP + (1 if earlier else 0)
    order = [(step - len(earlier), 2 * GROUP) for step in range(len(earlier))]
    order += [(step, block) for step in range(len(starts)) for block in range(blocks)]
    ahead = scores(*order[0])
    for i, (step, block) in enumerate(order):
        now = ahead
        if i + 1 < len(order):
            ahead = scores(*order[i + 1])
        if step == 0 and resumed and block < 2 * GROUP:
            state[block] = get_state(states[block // GROUP], block % GROUP)
        state[block] = absorb(state.get(block), now, loaded[step][0])
        if step == len(starts) - 1:
            if block < 2 * GROUP:
                put_state((keep, send)[block // GROUP], block % GROUP, state[block])
            else:
                for ref in (keep, send):
                    put_state(ref, GROUP, absorb_own(me, halves, beams, state[block]))


def beam_queries(me, mine, theirs):
    halves = [jnp.where(me == 0, mine[...], theirs[...]), jnp.where(me == 0, theirs[...], mine[...])]
    return halves, jnp.concatenate([h[: 8 * BEAMS] for h in halves], 0).astype(BF16)


def absorb_own(me, halves, queries, state):
    top, total, acc = state
    count = 4 * BEAMS
    pad = jnp.zeros((count - 3 * BEAMS, HEAD), F32)
    own_k = jnp.concatenate([halves[0][8 * BEAMS :], pad], 0).astype(BF16)
    own_v = jnp.concatenate([halves[1][8 * BEAMS :], pad], 0).astype(BF16)
    row = lax.broadcasted_iota(jnp.int32, (TOKENS, count), 0)
    key = lax.broadcasted_iota(jnp.int32, (TOKENS, count), 1)
    step = (row // (4 * BEAMS)) % 2
    beam = row % BEAMS
    slot = key // BEAMS
    first = jnp.logical_and(step == 0, slot == 0)
    second = jnp.logical_and(step == 1, jnp.logical_or(slot == 1, slot == 2))
    seen = jnp.logical_and(beam == key % BEAMS, jnp.logical_or(first, second))
    seen = jnp.logical_and(seen, beam // 4 == me)
    own = jnp.where(seen, dot_nt(queries, own_k), HIDE)
    peak = jnp.maximum(top, jnp.max(own, axis=-1, keepdims=True))
    alpha = jnp.exp2((top - peak) * EXP2_SCALE)
    w = jnp.exp2((own - peak[:, :1]) * EXP2_SCALE)
    total = total * alpha + jnp.sum(w, axis=-1, keepdims=True)
    acc = acc * alpha + dot_nn(w.astype(BF16), own_v)
    return peak, total, acc


def merge_kernel(core, keep, got, out, message):
    me = core[0]
    for zh in range(4):
        message[zh, NEW:, WIDTH:] = jnp.zeros((NEW, HEAD), F32)
    for slot in range(GROUP + 1):
        parts = [get_state(ref, slot) for ref in (keep, got)]
        peak = jnp.maximum(parts[0][0], parts[1][0])
        a, b = [jnp.exp2((p[0] - peak) * EXP2_SCALE) for p in parts]
        total = parts[0][1] * a + parts[1][1] * b
        mixed = (parts[0][2] * a + parts[1][2] * b) / total
        if slot < GROUP:
            lanes = slice(slot * HEAD, (slot + 1) * HEAD)
            for zh in range(4):
                message[zh, :, lanes] = mixed[zh * 2 * NEW : (zh + 1) * 2 * NEW]
        else:
            for block in range(16):
                half, step, head = block // 8, (block // 4) % 2, block % 4
                at = step * GROUP + half * 4 + head
                tile = mixed[block * BEAMS : (block + 1) * BEAMS]
                tile = jnp.where(me == 0, tile[:4], tile[4:])
                for zh in range(4):
                    message[zh, at : at + 1, WIDTH:] = tile[zh : zh + 1]
    out[...] = message[...].astype(BF16)


def place_kernel(core, near, far, stretch, decode):
    me = core[0]
    for j in range(2):
        lanes = slice(j * WIDTH, (j + 1) * WIDTH)
        own, other = near[2 * j + me], far[2 * j + me]
        for side, parity in ((own, me), (other, 1 - me)):
            for low in range(2):
                row = pl.multiple_of(low * 2 * NEW + parity * NEW, NEW)
                stretch[pl.ds(row, NEW), lanes] = side[low * NEW : (low + 1) * NEW, :WIDTH]
        tails = [v[:NEW, WIDTH:].astype(F32) for v in (own, other)]
        for parity in range(2):
            few = jnp.where(me == parity, tails[0], tails[1])
            steps = [
                jnp.concatenate([few[s * GROUP + g : s * GROUP + g + 1] for g in range(GROUP)], 1)
                for s in range(2)
            ]
            decode[parity, :, lanes] = jnp.concatenate(steps, 0).astype(BF16)


def shards(
    block_query_rows,
    block_key_rows,
    block_value_rows,
    stretch_pos,
    prompt_key_cache,
    prompt_value_cache,
    embed_table,
    query_weight,
    key_weight,
    value_weight,
    beam_tokens,
    parent_beam,
):
    xi, yi, ci = (lax.axis_index(a) for a in ("x", "y", "c"))
    core = jnp.stack([ci, xi * 4 + yi, xi, lax.axis_index(GRP)])
    core = core.astype(jnp.int32)

    depth = query_weight.shape[0]
    q_cols = query_weight.shape[1] // 4
    packed, *weights = call(
        pack_kernel,
        (
            jax.ShapeDtypeStruct((8, BOTH + 4 * NEW, 2 * HEAD), BF16),
            *[jax.ShapeDtypeStruct((depth, q_cols + HEAD), BF16)] * 4,
        ),
        (core,),
        (
            prompt_key_cache,
            prompt_value_cache,
            block_key_rows,
            block_value_rows,
            block_query_rows,
            query_weight,
            key_weight,
            value_weight,
        ),
        "pack",
    )
    packed = lax.all_to_all(packed, DEPTH, split_axis=0, concat_axis=0, tiled=True)

    def cross(v, axis, k):
        return lax.ppermute(v, axis, [(i, i ^ k) for i in range(4)])

    weights = [weights[0]] + [cross(weights[k], "x", k) for k in (1, 2, 3)]

    vocab_rows = embed_table.shape[0]
    beams = beam_tokens.shape[0]
    ids = jnp.transpose(beam_tokens.reshape(4, 4, 4, 2, 2), (4, 1, 2, 3, 0)).reshape(-1)
    looked = embed_table.at[ids % vocab_rows].get(mode="promise_in_bounds")
    looked = [looked] + [cross(looked, GRP, k) for k in (1, 2, 3)]
    weights, looked = lax.optimization_barrier((weights, looked))

    def swap(v, axis, turn):
        pairs = []
        for at in range(8):
            i, c = at // 2, at % 2
            pairs.append((at, (i ^ (1 if c == turn else 3)) * 2 + c))
        return lax.ppermute(v, (axis, "c"), pairs)

    halves = [packed[:4, :BOTH][None], packed[4:, :BOTH][None]]
    got = [swap(half, axis, 0) for half, axis in zip(halves, ("x", "y"))]
    got, looked = lax.optimization_barrier((got, looked))
    halves = [jnp.concatenate(pair, 0) for pair in zip(halves, got)]
    near = [
        jnp.concatenate([half, swap(half, axis, 1)], 0) for half, axis in zip(halves, ("x", "y"))
    ]
    packed_other = lax.ppermute(packed, "c", [(0, 1), (1, 0)])

    pos = jnp.transpose(stretch_pos.reshape(4, 4, 4, 2, 2, NEW), (4, 1, 2, 0, 3, 5))
    halves = lax.dynamic_index_in_dim(pos.reshape(2, 4, 4, 2, TOKENS // 2), ci, 0, keepdims=False)
    pos = pos.reshape(32, TOKENS)

    def met(table, axis, index):
        table = jnp.moveaxis(table, axis, 0)
        table = jnp.where(index % 2 == 1, jnp.concatenate([table[1:2], table[:1], table[3:], table[2:3]], 0), table)
        table = jnp.where(index // 2 == 1, jnp.concatenate([table[2:], table[:2]], 0), table)
        one, three = jnp.where(ci == 0, table[1], table[3]), jnp.where(ci == 0, table[3], table[1])
        return jnp.moveaxis(jnp.stack([table[0], one, three, table[2]]), 0, axis)

    halves = met(met(halves, 0, xi), 1, yi)
    line_pos = jnp.concatenate(
        [
            jnp.transpose(halves[:, :, 0], (1, 0, 2)).reshape(4, 2 * TOKENS),
            halves[:, :, 1].reshape(4, 2 * TOKENS),
        ],
        0,
    )

    hidden = call(
        hidden_kernel,
        jax.ShapeDtypeStruct((2 * beams, HEAD), BF16),
        (core,),
        ((ids // vocab_rows).reshape(-1, HEAD), *looked),
        "hidden",
    )
    hidden = [hidden] + [cross(hidden, "x", k) for k in (1, 2, 3)]

    near, hidden = lax.optimization_barrier((near, hidden))
    far = [swap(line, axis, 0) for line, axis in zip(near, ("y", "x"))]
    both = [jnp.concatenate(pair, 0) for pair in zip(near, far)]

    beam_id = np.arange(beams, dtype=np.int32).reshape(4, 4, 4, 2).transpose(1, 2, 3, 0)
    parent = jnp.transpose(parent_beam.reshape(4, 4, 4, 2), (1, 2, 3, 0))
    part = call(
        project_kernel,
        jax.ShapeDtypeStruct((16, TILES, HEAD), F32),
        (),
        (parent.reshape(1, -1), beam_id.reshape(1, -1), *hidden, *weights),
        "project",
        scratch=[
            pltpu.VMEM((2 * beams, q_cols + HEAD), F32),
            pltpu.VMEM((beams, HEAD), F32),
        ],
    )
    part, both = lax.optimization_barrier((part, both))
    rest = [swap(line, axis, 1) for line, axis in zip(both, ("y", "x"))]
    part = lax.all_to_all(part, ("zh", "y"), split_axis=0, concat_axis=0, tiled=True)
    def attend(starts, carry, pieces, name, earlier=(), beam_rows=()):
        work = 2 * GROUP * TOKENS * len(starts) * 32 * BOTH
        slots = GROUP + (1 if earlier else 0)
        state = jax.ShapeDtypeStruct((slots * TOKENS + STATS, HEAD), F32)
        return call(
            lambda *refs: attend_kernel(starts, bool(carry), earlier, *refs),
            (state, state),
            (core,),
            (pos, line_pos, packed, packed_other, *beam_rows, *carry, *pieces),
            name,
            cost=pl.CostEstimate(
                flops=8 * work * HEAD, bytes_accessed=work // 4, transcendentals=work
            ),
        )

    carry = attend(((0, 0, 0), (2, 0, 1)), (), near + far, "attend_near")
    carry, part = lax.optimization_barrier((carry, part))
    part = call(sum_kernel, jax.ShapeDtypeStruct((TILES, HEAD), F32), (), (part,), "sum")
    pairs = []
    for at in range(64):
        h, j, p, l, c = at >> 4, (at >> 3) & 1, (at >> 2) & 1, (at >> 1) & 1, at & 1
        pairs.append((at, (((2 * j + c) * 4 + h) * 2 + l) * 2 + p))
    mine = lax.ppermute(part, ("zh", "x", "zl", "c"), pairs)
    sides = (mine, lax.ppermute(mine, "c", [(0, 1), (1, 0)]))
    keep, send = attend(
        ((4, 0, 2), (4, 1, 3)),
        carry,
        near + far + rest,
        "attend_rest",
        earlier=((0, 0, 0), (2, 0, 1)),
        beam_rows=sides,
    )
    got = lax.ppermute(send, "c", [(0, 1), (1, 0)])
    messages = call(
        merge_kernel,
        jax.ShapeDtypeStruct((4, 2 * NEW, MESSAGE), BF16),
        (core,),
        (keep, got),
        "merge",
        scratch=[pltpu.VMEM((4, 2 * NEW, MESSAGE), F32)],
    )

    near = lax.all_to_all(messages, "zh", split_axis=0, concat_axis=0, tiled=True)
    far = lax.ppermute(near, "c", [(0, 1), (1, 0)])
    return call(
        place_kernel,
        (
            jax.ShapeDtypeStruct((4 * NEW, 2 * WIDTH), BF16),
            jax.ShapeDtypeStruct((2, 2, 2 * WIDTH), BF16),
        ),
        (core,),
        (near, far),
        "place",
    )


def solution(mesh):
    fine = Mesh(mesh.devices.reshape(4, 4, 4, 2, 2), ALL)
    return jax.shard_map(
        shards,
        mesh=fine,
        in_specs=(
            P(ALL, None),
            P(ALL, None),
            P(ALL, None),
            P(),
            P(ALL, None),
            P(ALL, None),
            P(GRP, SEQ),
            P(SEQ, GRP),
            P(SEQ, GRP),
            P(SEQ, GRP),
            P(),
            P(),
        ),
        out_specs=(P(SEQ, GRP), P(SEQ, None, GRP)),
        check_vma=False,
    )
```

```python
import jax
import jax.numpy as jnp
import numpy as np
from jax import lax
from jax.experimental import pallas as pl
from jax.experimental.pallas import tpu as pltpu
from jax.sharding import Mesh, PartitionSpec as P

HEAD = 128
GROUP = 8
WIDTH = GROUP * HEAD
EXP2_SCALE = HEAD ** (-0.5) * 1.4426950408889634
HIDE = -1e30
ALL = ("zh", "x", "y", "zl", "c")
SEQ = ("zh", "x", "y")
GRP = ("zl", "c")
DEPTH = ("zh", "zl")
OLD, NEW = 32, 16
BOTH = OLD + NEW
TOKENS = 8 * NEW
BEAMS = 8
TILES = 11 * BEAMS
STATS = 32
MESSAGE = WIDTH + HEAD
VMEM = pltpu.CompilerParams(vmem_limit_bytes=56 * 1024 * 1024)
SMEM_SPEC = pl.BlockSpec(memory_space=pltpu.SMEM)
VMEM_SPEC = pl.BlockSpec(memory_space=pltpu.VMEM)
BF16, F32 = jnp.bfloat16, jnp.float32


def dot_nt(a, b):
    return lax.dot_general(a, b, (((1,), (1,)), ((), ())), preferred_element_type=F32)


def dot_nn(a, b):
    return lax.dot_general(a, b, (((1,), (0,)), ((), ())), preferred_element_type=F32)


def call(kernel, out_shape, scalars, args, name, cost=None, scratch=()):
    return pl.pallas_call(
        kernel,
        out_shape=out_shape,
        in_specs=[SMEM_SPEC] * len(scalars) + [VMEM_SPEC] * len(args),
        out_specs=jax.tree.map(lambda _: VMEM_SPEC, out_shape),
        scratch_shapes=list(scratch),
        cost_estimate=cost,
        compiler_params=VMEM,
        name=name,
    )(*scalars, *args)


def head_of(plane):
    return 4 * (plane & 1) + 2 * ((plane >> 1) & 1) + (plane >> 2)


def pack_kernel(core, old_k, old_v, new_k, new_v, q, wq, wk, wv, out, *w_out):
    for plane in range(8):
        head = head_of(plane)
        cols = slice(head * HEAD, (head + 1) * HEAD)
        out[plane, :OLD, :HEAD] = old_k[:, cols]
        out[plane, :OLD, HEAD:] = old_v[:, cols]
        out[plane, OLD:BOTH, :HEAD] = new_k[:, cols]
        out[plane, OLD:BOTH, HEAD:] = new_v[:, cols]
        for pair in range(4):
            at = head * WIDTH + pair * 2 * HEAD
            out[plane, BOTH + pair * NEW : BOTH + (pair + 1) * NEW, :] = q[:, at : at + 2 * HEAD]
    for k in range(4):
        part = core[2] ^ k
        w_out[k][:, : 4 * HEAD] = wq[:, pl.ds(pl.multiple_of(part * 4 * HEAD, 4 * HEAD), 4 * HEAD)]
        cols = pl.ds(pl.multiple_of((part // 2) * HEAD, HEAD), HEAD)
        w_out[k][:, 4 * HEAD :] = jnp.where(part % 2 == 0, wk[:, cols], wv[:, cols])


def spread(ref, row):
    return jnp.transpose(jnp.broadcast_to(ref[row : row + 1, :].astype(F32), (TOKENS, HEAD)))


def hidden_kernel(core, owner, *refs):
    looked, out = refs[:4], refs[4]
    for part in range(owner.shape[0]):
        at = slice(part * HEAD, (part + 1) * HEAD)
        who = spread(owner, part)
        rows = jnp.zeros((HEAD, HEAD), F32)
        for k in range(4):
            from_k = (core[3] ^ k).astype(F32)
            rows = rows + jnp.where(who == from_k, looked[k][at, :].astype(F32), 0.0)
        out[at, :] = rows.astype(BF16)


def project_kernel(parent, beam_id, *refs):
    hidden, weights, (out, total, extra) = refs[:4], refs[4:8], refs[8:]
    beams = extra.shape[0]
    pick = jnp.where(spread(parent, 0) == beam_id[...].astype(F32), 1.0, 0.0).astype(BF16)
    acc = acc_extra = 0.0
    for k in range(4):
        rows = hidden[k][...]
        acc = acc + dot_nn(rows, weights[k][...])
        chosen = dot_nn(pick, rows[:beams]).astype(BF16)
        acc_extra = acc_extra + dot_nn(chosen, weights[k][:, 4 * HEAD :])
    total[...] = acc
    extra[...] = acc_extra
    for chip in range(16):
        for step in range(2):
            rows = slice(step * beams + chip * BEAMS, step * beams + (chip + 1) * BEAMS)
            for head in range(4):
                at = (step * 4 + head) * BEAMS
                out[chip, at : at + BEAMS, :] = total[rows, head * HEAD : (head + 1) * HEAD]
            at = (8 + step) * BEAMS
            out[chip, at : at + BEAMS, :] = total[rows, 4 * HEAD :]
        out[chip, 10 * BEAMS :, :] = extra[chip * BEAMS : (chip + 1) * BEAMS, :]


def sum_kernel(parts, out):
    terms = [parts[i] for i in range(parts.shape[0])]
    while len(terms) > 1:
        terms = [a + b for a, b in zip(terms[::2], terms[1::2])]
    out[...] = terms[0]


def load_lines(pair):
    wide = []
    for low, high in ((0, OLD), (OLD, BOTH)):
        count = 16 * (high - low)
        k = jnp.concatenate([r[:, :, low:high, :HEAD].reshape(count, HEAD) for r in pair], 0)
        v = jnp.concatenate([r[:, :, low:high, HEAD:].reshape(count, HEAD) for r in pair], 0)
        wide.append((k, jnp.concatenate([v, jnp.ones_like(v)], 1)))
    return wide


def absorb(state, tiles, wide):
    peak = jnp.maximum(
        jnp.max(tiles[0], axis=-1, keepdims=True), jnp.max(tiles[1], axis=-1, keepdims=True)
    )
    if state is None:
        peak = jnp.broadcast_to(peak, (TOKENS, HEAD))
    else:
        top, total, acc = state
        peak = jnp.maximum(top, peak)
        alpha = jnp.exp2((top - peak) * EXP2_SCALE)
    mixed = 0.0
    for s, (_, v) in zip(tiles, wide):
        w = jnp.exp2((s - peak[:, :1]) * EXP2_SCALE).astype(BF16)
        mixed = mixed + dot_nn(w, v)
    if state is None:
        return peak, mixed[:, HEAD:], mixed[:, :HEAD]
    return peak, mixed[:, HEAD:] + total * alpha, mixed[:, :HEAD] + acc * alpha


def put_state(ref, slot, state):
    top, total, acc = state
    ref[slot * TOKENS : (slot + 1) * TOKENS, :] = acc
    at = ref.shape[0] - STATS + slot
    ref[at : at + 1, :] = jnp.transpose(top)[:1]
    at = at + STATS // 2
    ref[at : at + 1, :] = jnp.transpose(total)[:1]


def get_state(ref, slot):
    at = ref.shape[0] - STATS + slot
    rows = slice(slot * TOKENS, (slot + 1) * TOKENS)
    return spread(ref, at), spread(ref, at + STATS // 2), ref[rows, :]


def attend_kernel(starts, resumed, earlier, core, pos, lines, own, other, *refs):
    if earlier:
        mine, theirs, refs = refs[0], refs[1], refs[2:]
    if resumed:
        states, refs = refs[:2], refs[2:]
    kv, (keep, send) = refs[:-2], refs[-2:]
    me, place = core[0], core[1]

    def column(which):
        row = pos[pl.ds(which * 16 + place, 1), :].astype(F32)
        return jnp.transpose(jnp.broadcast_to(row, (TOKENS, HEAD)))[:, :1]

    qpos = (column(me), column(1 - me))
    loaded = {}
    if earlier:
        halves, beams = beam_queries(me, mine, theirs)

    def scores(step, block):
        if step not in loaded and step < 0:
            first, part, _ = earlier[step]
            pair = [r.at[4 * part : 4 * part + 4] for r in kv[first : first + 2]]
            loaded[step] = (load_lines(pair), None)
        if step not in loaded:
            first, part, line = starts[step]
            kpos = jnp.concatenate([lines[line : line + 1], lines[4 + line : 5 + line]], 1)
            kpos = kpos.astype(F32)
            bias = [jnp.where(kpos <= p, 0.0, HIDE) for p in qpos]
            pair = [r.at[4 * part : 4 * part + 4] for r in kv[first : first + 2]]
            loaded[step] = (load_lines(pair), bias)
        wide, bias = loaded[step]
        if block == 2 * GROUP:
            return [dot_nt(beams, k) for k, _ in wide]
        head = block % GROUP
        lanes = slice((head % 2) * HEAD, (head % 2 + 1) * HEAD)
        at = BOTH + (head // 2) * NEW
        q = (own, other)[block // GROUP][:, at : at + NEW, lanes].reshape(TOKENS, HEAD)
        return dot_nt(q, wide[0][0]), dot_nt(q, wide[1][0]) + bias[block // GROUP]

    state = {}
    blocks = 2 * GROUP + (1 if earlier else 0)
    order = [(step - len(earlier), 2 * GROUP) for step in range(len(earlier))]
    order += [(step, block) for step in range(len(starts)) for block in range(blocks)]
    ahead = scores(*order[0])
    for i, (step, block) in enumerate(order):
        now = ahead
        if i + 1 < len(order):
            ahead = scores(*order[i + 1])
        if step == 0 and resumed and block < 2 * GROUP:
            state[block] = get_state(states[block // GROUP], block % GROUP)
        state[block] = absorb(state.get(block), now, loaded[step][0])
        if step == len(starts) - 1:
            if block < 2 * GROUP:
                put_state((keep, send)[block // GROUP], block % GROUP, state[block])
            else:
                for ref in (keep, send):
                    put_state(ref, GROUP, absorb_own(me, halves, beams, state[block]))


def beam_queries(me, mine, theirs):
    halves = [jnp.where(me == 0, mine[...], theirs[...]), jnp.where(me == 0, theirs[...], mine[...])]
    return halves, jnp.concatenate([h[: 8 * BEAMS] for h in halves], 0).astype(BF16)


def absorb_own(me, halves, queries, state):
    top, total, acc = state
    count = 4 * BEAMS
    pad = jnp.zeros((count - 3 * BEAMS, HEAD), F32)
    own_k = jnp.concatenate([halves[0][8 * BEAMS :], pad], 0).astype(BF16)
    own_v = jnp.concatenate([halves[1][8 * BEAMS :], pad], 0).astype(BF16)
    row = lax.broadcasted_iota(jnp.int32, (TOKENS, count), 0)
    key = lax.broadcasted_iota(jnp.int32, (TOKENS, count), 1)
    step = (row // (4 * BEAMS)) % 2
    beam = row % BEAMS
    slot = key // BEAMS
    first = jnp.logical_and(step == 0, slot == 0)
    second = jnp.logical_and(step == 1, jnp.logical_or(slot == 1, slot == 2))
    seen = jnp.logical_and(beam == key % BEAMS, jnp.logical_or(first, second))
    seen = jnp.logical_and(seen, beam // 4 == me)
    own = jnp.where(seen, dot_nt(queries, own_k), HIDE)
    peak = jnp.maximum(top, jnp.max(own, axis=-1, keepdims=True))
    alpha = jnp.exp2((top - peak) * EXP2_SCALE)
    w = jnp.exp2((own - peak[:, :1]) * EXP2_SCALE)
    total = total * alpha + jnp.sum(w, axis=-1, keepdims=True)
    acc = acc * alpha + dot_nn(w.astype(BF16), own_v)
    return peak, total, acc


def merge_kernel(core, keep, got, out, message):
    me = core[0]
    for zh in range(4):
        message[zh, NEW:, WIDTH:] = jnp.zeros((NEW, HEAD), F32)
    for slot in range(GROUP + 1):
        parts = [get_state(ref, slot) for ref in (keep, got)]
        peak = jnp.maximum(parts[0][0], parts[1][0])
        a, b = [jnp.exp2((p[0] - peak) * EXP2_SCALE) for p in parts]
        total = parts[0][1] * a + parts[1][1] * b
        mixed = (parts[0][2] * a + parts[1][2] * b) / total
        if slot < GROUP:
            lanes = slice(slot * HEAD, (slot + 1) * HEAD)
            for zh in range(4):
                message[zh, :, lanes] = mixed[zh * 2 * NEW : (zh + 1) * 2 * NEW]
        else:
            for block in range(16):
                half, step, head = block // 8, (block // 4) % 2, block % 4
                at = step * GROUP + half * 4 + head
                tile = mixed[block * BEAMS : (block + 1) * BEAMS]
                tile = jnp.where(me == 0, tile[:4], tile[4:])
                for zh in range(4):
                    message[zh, at : at + 1, WIDTH:] = tile[zh : zh + 1]
    out[...] = message[...].astype(BF16)


def place_kernel(core, near, far, stretch, decode):
    me = core[0]
    for j in range(2):
        lanes = slice(j * WIDTH, (j + 1) * WIDTH)
        own, other = near[2 * j + me], far[2 * j + me]
        for side, parity in ((own, me), (other, 1 - me)):
            for low in range(2):
                row = pl.multiple_of(low * 2 * NEW + parity * NEW, NEW)
                stretch[pl.ds(row, NEW), lanes] = side[low * NEW : (low + 1) * NEW, :WIDTH]
        tails = [v[:NEW, WIDTH:].astype(F32) for v in (own, other)]
        for parity in range(2):
            few = jnp.where(me == parity, tails[0], tails[1])
            steps = [
                jnp.concatenate([few[s * GROUP + g : s * GROUP + g + 1] for g in range(GROUP)], 1)
                for s in range(2)
            ]
            decode[parity, :, lanes] = jnp.concatenate(steps, 0).astype(BF16)


def shards(
    block_query_rows,
    block_key_rows,
    block_value_rows,
    stretch_pos,
    prompt_key_cache,
    prompt_value_cache,
    embed_table,
    query_weight,
    key_weight,
    value_weight,
    beam_tokens,
    parent_beam,
):
    xi, yi, ci = (lax.axis_index(a) for a in ("x", "y", "c"))
    core = jnp.stack([ci, xi * 4 + yi, xi, lax.axis_index(GRP)])
    core = core.astype(jnp.int32)

    depth = query_weight.shape[0]
    q_cols = query_weight.shape[1] // 4
    packed, *weights = call(
        pack_kernel,
        (
            jax.ShapeDtypeStruct((8, BOTH + 4 * NEW, 2 * HEAD), BF16),
            *[jax.ShapeDtypeStruct((depth, q_cols + HEAD), BF16)] * 4,
        ),
        (core,),
        (
            prompt_key_cache,
            prompt_value_cache,
            block_key_rows,
            block_value_rows,
            block_query_rows,
            query_weight,
            key_weight,
            value_weight,
        ),
        "pack",
    )
    packed = lax.all_to_all(packed, DEPTH, split_axis=0, concat_axis=0, tiled=True)

    def cross(v, axis, k):
        return lax.ppermute(v, axis, [(i, i ^ k) for i in range(4)])

    weights = [weights[0]] + [cross(weights[k], "x", k) for k in (1, 2, 3)]

    vocab_rows = embed_table.shape[0]
    beams = beam_tokens.shape[0]
    ids = jnp.transpose(beam_tokens.reshape(4, 4, 4, 2, 2), (4, 1, 2, 3, 0)).reshape(-1)
    looked = embed_table.at[ids % vocab_rows].get(mode="promise_in_bounds")
    looked = [looked] + [cross(looked, GRP, k) for k in (1, 2, 3)]
    weights, looked = lax.optimization_barrier((weights, looked))

    def swap(v, axis, turn):
        pairs = []
        for at in range(8):
            i, c = at // 2, at % 2
            pairs.append((at, (i ^ (1 if c == turn else 3)) * 2 + c))
        return lax.ppermute(v, (axis, "c"), pairs)

    halves = [packed[:4, :BOTH][None], packed[4:, :BOTH][None]]
    got = [swap(half, axis, 0) for half, axis in zip(halves, ("x", "y"))]
    got, looked = lax.optimization_barrier((got, looked))
    halves = [jnp.concatenate(pair, 0) for pair in zip(halves, got)]
    near = [
        jnp.concatenate([half, swap(half, axis, 1)], 0) for half, axis in zip(halves, ("x", "y"))
    ]
    packed_other = lax.ppermute(packed, "c", [(0, 1), (1, 0)])

    pos = jnp.transpose(stretch_pos.reshape(4, 4, 4, 2, 2, NEW), (4, 1, 2, 0, 3, 5))
    halves = lax.dynamic_index_in_dim(pos.reshape(2, 4, 4, 2, TOKENS // 2), ci, 0, keepdims=False)
    pos = pos.reshape(32, TOKENS)

    def met(table, axis, index):
        table = jnp.moveaxis(table, axis, 0)
        table = jnp.where(index % 2 == 1, jnp.concatenate([table[1:2], table[:1], table[3:], table[2:3]], 0), table)
        table = jnp.where(index // 2 == 1, jnp.concatenate([table[2:], table[:2]], 0), table)
        one, three = jnp.where(ci == 0, table[1], table[3]), jnp.where(ci == 0, table[3], table[1])
        return jnp.moveaxis(jnp.stack([table[0], one, three, table[2]]), 0, axis)

    halves = met(met(halves, 0, xi), 1, yi)
    line_pos = jnp.concatenate(
        [
            jnp.transpose(halves[:, :, 0], (1, 0, 2)).reshape(4, 2 * TOKENS),
            halves[:, :, 1].reshape(4, 2 * TOKENS),
        ],
        0,
    )

    hidden = call(
        hidden_kernel,
        jax.ShapeDtypeStruct((2 * beams, HEAD), BF16),
        (core,),
        ((ids // vocab_rows).reshape(-1, HEAD), *looked),
        "hidden",
    )
    hidden = [hidden] + [cross(hidden, "x", k) for k in (1, 2, 3)]

    near, hidden = lax.optimization_barrier((near, hidden))
    far = [swap(line, axis, 0) for line, axis in zip(near, ("y", "x"))]
    both = [jnp.concatenate(pair, 0) for pair in zip(near, far)]

    beam_id = np.arange(beams, dtype=np.int32).reshape(4, 4, 4, 2).transpose(1, 2, 3, 0)
    parent = jnp.transpose(parent_beam.reshape(4, 4, 4, 2), (1, 2, 3, 0))
    part = call(
        project_kernel,
        jax.ShapeDtypeStruct((16, TILES, HEAD), F32),
        (),
        (parent.reshape(1, -1), beam_id.reshape(1, -1), *hidden, *weights),
        "project",
        scratch=[
            pltpu.VMEM((2 * beams, q_cols + HEAD), F32),
            pltpu.VMEM((beams, HEAD), F32),
        ],
    )
    part, both = lax.optimization_barrier((part, both))
    rest = [swap(line, axis, 1) for line, axis in zip(both, ("y", "x"))]
    part = lax.all_to_all(part, ("zh", "y"), split_axis=0, concat_axis=0, tiled=True)
    def attend(starts, carry, pieces, name, earlier=(), beam_rows=()):
        work = 2 * GROUP * TOKENS * len(starts) * 32 * BOTH
        slots = GROUP + (1 if earlier else 0)
        state = jax.ShapeDtypeStruct((slots * TOKENS + STATS, HEAD), F32)
        return call(
            lambda *refs: attend_kernel(starts, bool(carry), earlier, *refs),
            (state, state),
            (core,),
            (pos, line_pos, packed, packed_other, *beam_rows, *carry, *pieces),
            name,
            cost=pl.CostEstimate(
                flops=8 * work * HEAD, bytes_accessed=work // 4, transcendentals=work
            ),
        )

    carry = attend(((0, 0, 0),), (), near, "attend_near")
    carry, part = lax.optimization_barrier((carry, part))
    part = call(sum_kernel, jax.ShapeDtypeStruct((TILES, HEAD), F32), (), (part,), "sum")
    pairs = []
    for at in range(64):
        h, j, p, l, c = at >> 4, (at >> 3) & 1, (at >> 2) & 1, (at >> 1) & 1, at & 1
        pairs.append((at, (((2 * j + c) * 4 + h) * 2 + l) * 2 + p))
    mine = lax.ppermute(part, ("zh", "x", "zl", "c"), pairs)
    sides = (mine, lax.ppermute(mine, "c", [(0, 1), (1, 0)]))
    carry = attend(((0, 0, 1),), carry, far, "attend_far")
    keep, send = attend(
        ((4, 0, 2), (4, 1, 3)),
        carry,
        near + far + rest,
        "attend_rest",
        earlier=((0, 0, 0), (2, 0, 1)),
        beam_rows=sides,
    )
    got = lax.ppermute(send, "c", [(0, 1), (1, 0)])
    messages = call(
        merge_kernel,
        jax.ShapeDtypeStruct((4, 2 * NEW, MESSAGE), BF16),
        (core,),
        (keep, got),
        "merge",
        scratch=[pltpu.VMEM((4, 2 * NEW, MESSAGE), F32)],
    )

    near = lax.all_to_all(messages, "zh", split_axis=0, concat_axis=0, tiled=True)
    far = lax.ppermute(near, "c", [(0, 1), (1, 0)])
    return call(
        place_kernel,
        (
            jax.ShapeDtypeStruct((4 * NEW, 2 * WIDTH), BF16),
            jax.ShapeDtypeStruct((2, 2, 2 * WIDTH), BF16),
        ),
        (core,),
        (near, far),
        "place",
    )


def solution(mesh):
    fine = Mesh(mesh.devices.reshape(4, 4, 4, 2, 2), ALL)
    return jax.shard_map(
        shards,
        mesh=fine,
        in_specs=(
            P(ALL, None),
            P(ALL, None),
            P(ALL, None),
            P(),
            P(ALL, None),
            P(ALL, None),
            P(GRP, SEQ),
            P(SEQ, GRP),
            P(SEQ, GRP),
            P(SEQ, GRP),
            P(),
            P(),
        ),
        out_specs=(P(SEQ, GRP), P(SEQ, None, GRP)),
        check_vma=False,
    )
```
